256 devices in a mesh: section: 16 (over x_hi, y, core), dp: 16 (over x_lo, z).
Axes of the slice: x: 4 (x_hi: 2, x_lo: 2; x = x_hi * 2 + x_lo), y: 4, z: 8, core: 2. Of those that a mesh axis runs over, the one named last changes fastest.
Arguments:
- micro_inputs: bfloat16 [2, 4, 256, 8192], P(None, None, 'dp'), may hold values from -6 to 6
- cotangent: bfloat16 [2, 4, 256, 8192], P(None, None, 'dp'), may hold values from -6 to 6
- norm_gain: bfloat16 [16, 8192], P('section'), may hold values from 0.5 to 1.5
- enter_weight: float32 [16, 8192, 128], P('section', 'dp'), may hold values from -0.0625 to 0.0625
- enter_moment: float32 [16, 8192, 128], P('section', 'dp'), may hold values from -150 to 150
- enter_second: float32 [16, 8192, 128], P('section', 'dp'), may hold values from 1000 to 100000
- leave_weight: float32 [16, 128, 8192], P('section', None, 'dp'), may hold values from -0.5 to 0.5
- leave_moment: float32 [16, 128, 8192], P('section', None, 'dp'), may hold values from -12 to 12
- leave_second: float32 [16, 128, 8192], P('section', None, 'dp'), may hold values from 10 to 1000
Outputs:
- new_enter_weight: float32 [16, 8192, 128], P('section', 'dp')
- new_enter_moment: float32 [16, 8192, 128], P('section', 'dp')
- new_enter_second: float32 [16, 8192, 128], P('section', 'dp')
- new_leave_weight: float32 [16, 128, 8192], P('section', None, 'dp')
- new_leave_moment: float32 [16, 128, 8192], P('section', None, 'dp')
- new_leave_second: float32 [16, 128, 8192], P('section', None, 'dp')
The draws below stay inside these ranges and needn't reach their ends.
All inputs are finite; a program needn't handle non-finite values.
Results may differ from the reference program's by a relative error of at most 0.04.
Values may be sent and summed in bfloat16 or wider, within the bound.
No kernel may reach another device: no remote copies, remote signals or barrier semaphores. Data moves between devices by JAX's collectives and lax.ppermute only.
A program may use at most 64 MiB of HBM per device.

```python
import math
import jax
import jax.numpy as jnp
from jax import lax

D = 8192
RANK = 128
MB = 16
M = 4
ROWS = 256
LAYERS = 16
N_DP = 16


def steps_of(rng, shape, split, smallest, high):
    loudness, own = 1.0, jax.random.fold_in(rng, 6)
    for axis_at, blocks in split:
        steps = jnp.exp(jax.random.uniform(jax.random.fold_in(own, axis_at), (blocks,), jnp.float32, smallest / len(split), high / len(split)))
        loudness = loudness * jnp.repeat(steps, shape[axis_at] // blocks).reshape([-1 if axis == axis_at else 1 for axis in range(len(shape))])
    return loudness


def scatter_about(stream_key, extent, spread, bound, cuts=(), held_as=jnp.bfloat16):
    drawn = spread * jax.random.normal(stream_key, extent, jnp.float32)
    if cuts:
        drawn = drawn * steps_of(stream_key, extent, cuts, -0.22, 0.18)
    return jnp.clip(drawn, -bound, bound).astype(held_as)


def setup_inputs(seed: int = 0) -> dict:
    keys = jax.random.split(jax.random.key(seed), 10)
    return {
        "micro_inputs": scatter_about(keys[0], (2, M, ROWS, D), 1.0, 6.0, ((2, 16),)),
        "cotangent": scatter_about(keys[1], (2, M, ROWS, D), 1.0, 6.0, ((2, 16),)),
        "norm_gain": jnp.clip(1.0 + 0.1 * jax.random.normal(keys[2], (LAYERS, D), jnp.float32), 0.5, 1.5).astype(jnp.bfloat16),
        "enter_weight": scatter_about(keys[3], (LAYERS, D, RANK), D ** -0.5, 0.0625, ((0, 16), (1, 16)), jnp.float32),
        "enter_moment": scatter_about(keys[4], (LAYERS, D, RANK), 25.0, 150.0, ((0, 16), (1, 16)), jnp.float32),
        "enter_second": jnp.clip(jnp.exp(math.log(100000.0) - 4.6051702 * jax.random.uniform(keys[5], (LAYERS, D, RANK), jnp.float32) ** steps_of(keys[5], (LAYERS, D, RANK), ((0, 16), (1, 16)), -0.2, 0.2)), 1000.0, 100000.0),
        "leave_weight": scatter_about(keys[6], (LAYERS, RANK, D), RANK ** -0.5, 0.5, ((0, 16), (2, 16)), jnp.float32),
        "leave_moment": scatter_about(keys[7], (LAYERS, RANK, D), 2.0, 12.0, ((0, 16), (2, 16)), jnp.float32),
        "leave_second": jnp.clip(jnp.exp(math.log(1000.0) - 4.6051702 * jax.random.uniform(keys[8], (LAYERS, RANK, D), jnp.float32) ** steps_of(keys[8], (LAYERS, RANK, D), ((0, 16), (2, 16)), -0.2, 0.2)), 10.0, 1000.0),
    }


eps_norm = 1e-05
rate = 0.001
beta_one = 0.9
beta_two = 0.95
adam_eps = 1e-08
step_count = 10

def layer_inner(layer_rows, enter_mat, gain_row):
    wide_rows = layer_rows.astype(jnp.float32)
    inverse = lax.rsqrt(lax.optimization_barrier(jnp.mean(wide_rows * wide_rows, axis=-1, keepdims=True)) + eps_norm)
    normed = (wide_rows * inverse * gain_row.astype(jnp.float32)).astype(jnp.bfloat16)
    pre_act = jnp.dot(normed, enter_mat, preferred_element_type=jnp.float32)
    return (wide_rows, inverse, normed, pre_act)

def layer_forward(layer_rows, enter_mat, leave_mat, gain_row):
    wide_rows, inverse, normed, pre_act = layer_inner(layer_rows, enter_mat, gain_row)
    hidden = jax.nn.silu(pre_act).astype(jnp.bfloat16)
    branch = jnp.dot(hidden, leave_mat, preferred_element_type=jnp.float32)
    return (wide_rows + branch).astype(jnp.bfloat16)

def layer_backward(layer_rows, incoming, enter_mat, leave_mat, gain_row):
    wide_rows, inverse, normed, pre_act = layer_inner(layer_rows, enter_mat, gain_row)
    hidden_grad = lax.dot_general(incoming, leave_mat, (((1,), (1,)), ((), ())), preferred_element_type=jnp.float32)
    sig_act = jax.nn.sigmoid(pre_act)
    inner_grad = (hidden_grad * sig_act * (1.0 + pre_act * (1.0 - sig_act))).astype(jnp.bfloat16)
    normed_grad = lax.dot_general(inner_grad, enter_mat, (((1,), (1,)), ((), ())), preferred_element_type=jnp.float32)
    scaled = normed_grad * gain_row.astype(jnp.float32)
    mean_term = lax.optimization_barrier(jnp.mean(scaled * wide_rows, axis=-1, keepdims=True))
    outgoing = incoming.astype(jnp.float32) + inverse * scaled - wide_rows * (inverse * inverse * inverse) * mean_term
    return (outgoing.astype(jnp.bfloat16), inner_grad)

def adam_update(weight, moment, second, grad):
    moment_new = beta_one * moment + (1.0 - beta_one) * grad
    second_new = beta_two * second + (1.0 - beta_two) * grad * grad
    corr_one = 1.0 - beta_one ** step_count
    corr_two = 1.0 - beta_two ** step_count
    weight_new = weight - rate * (moment_new / corr_one) / (jnp.sqrt(second_new / corr_two) + adam_eps)
    return (weight_new, moment_new, second_new)

def grouped(values_in):
    return values_in.reshape(2, M, N_DP, MB, values_in.shape[-1]).astype(jnp.float32)

def merge_parts(part_sums):
    rounded = lax.optimization_barrier(part_sums.astype(jnp.bfloat16))
    return lax.optimization_barrier(jnp.sum(rounded.astype(jnp.float32), axis=(0, 1)))

def reference(micro_inputs, cotangent, norm_gain, enter_weight, enter_moment, enter_second, leave_weight, leave_moment, leave_second):
    enter_half = enter_weight.astype(jnp.bfloat16)
    leave_half = leave_weight.astype(jnp.bfloat16)
    flat_inputs = micro_inputs.reshape(-1, D)

    def forward_step(layer_rows, params):
        enter_mat, leave_mat, gain_row = params
        return (layer_forward(layer_rows, enter_mat, leave_mat, gain_row), layer_rows)
    final_rows, saved_rows = lax.scan(forward_step, flat_inputs, (enter_half, leave_half, norm_gain))

    def backward_step(incoming, params):
        layer_rows, enter_mat, leave_mat, gain_row = params
        outgoing, inner_grad = layer_backward(layer_rows, incoming, enter_mat, leave_mat, gain_row)
        wide_rows, inverse, normed, pre_act = layer_inner(layer_rows, enter_mat, gain_row)
        hidden = jax.nn.silu(pre_act).astype(jnp.bfloat16)
        enter_part = jnp.einsum('dmgrk,dmgrj->dgkj', grouped(normed), grouped(inner_grad))
        leave_part = jnp.einsum('dmgrj,dmgrk->dgjk', grouped(hidden), grouped(incoming))
        return (outgoing, (merge_parts(enter_part), merge_parts(leave_part)))
    first_grad, grads = lax.scan(backward_step, cotangent.reshape(-1, D), (saved_rows, enter_half, leave_half, norm_gain), reverse=True)
    enter_grad, leave_grad = grads
    new_enter, new_enter_moment, new_enter_second = adam_update(enter_weight, enter_moment, enter_second, enter_grad)
    new_leave, new_leave_moment, new_leave_second = adam_update(leave_weight, leave_moment, leave_second, leave_grad)
    return (new_enter, new_enter_moment, new_enter_second, new_leave, new_leave_moment, new_leave_second)
```

```python
import jax
import jax.numpy as jnp
from jax import lax
from jax.experimental import pallas as pl
from jax.experimental.pallas import tpu as pltpu
from jax.sharding import Mesh, PartitionSpec as P

eps_norm = 1e-05
rate = 0.001
beta_one = 0.9
beta_two = 0.95
adam_eps = 1e-08
step_count = 10

LAYERS = 16
RANK = 128
WIDTH = 8192
PARTS = 16
SLICE = WIDTH // PARTS
CHUNK = 128
REACH = LAYERS // 2 + 1
EXTRA = 16

SECTION = ("xh", "y", "c")
DP = ("xl", "z")

BF = jnp.bfloat16
F32 = jnp.float32


def nn(a, b):
    return lax.dot_general(a, b, (((1,), (0,)), ((), ())), preferred_element_type=F32)


def nt(a, b):
    return lax.dot_general(a, b, (((1,), (1,)), ((), ())), preferred_element_type=F32)


def tn(a, b):
    return lax.dot_general(a, b, (((0,), (0,)), ((), ())), preferred_element_type=F32)


def adam_update(weight, moment, second, grad):
    moment_new = beta_one * moment + (1.0 - beta_one) * grad
    second_new = beta_two * second + (1.0 - beta_two) * grad * grad
    corr_one = 1.0 - beta_one**step_count
    corr_two = 1.0 - beta_two**step_count
    weight_new = weight - rate * (moment_new / corr_one) / (
        jnp.sqrt(second_new / corr_two) + adam_eps
    )
    return (weight_new, moment_new, second_new)


def gram_kernel(index_ref, weights_ref, out_ref):
    section = index_ref[0]
    for reach in range(REACH):
        other = lax.rem(section + reach, LAYERS)
        low = jnp.minimum(section, other)
        high = jnp.maximum(section, other)
        block = nt(weights_ref[low, RANK:, :], weights_ref[high]).astype(BF)
        out_ref[2 * reach] = block[:, :RANK]
        out_ref[2 * reach + 1] = block[:, RANK:]


def gram_blocks(section, weights):
    return pl.pallas_call(
        gram_kernel,
        out_shape=jax.ShapeDtypeStruct((2 * REACH, RANK, RANK), BF),
        in_specs=[
            pl.BlockSpec(memory_space=pltpu.SMEM),
            pl.BlockSpec(memory_space=pltpu.VMEM),
        ],
        out_specs=pl.BlockSpec(memory_space=pltpu.VMEM),
        compiler_params=pltpu.CompilerParams(vmem_limit_bytes=32 * 2**20),
        cost_estimate=pl.CostEstimate(
            flops=2 * REACH * RANK * 2 * RANK * SLICE, bytes_accessed=5 * 2**20, transcendentals=0
        ),
    )(section.reshape(1), weights)


def project_kernel(rows_ref, grads_ref, extra_ref, weights_ref, out_ref):
    rows = rows_ref[...]
    grads = grads_ref[...]
    for layer in range(LAYERS):
        out_ref[layer, :CHUNK, : 2 * RANK] = nt(rows, weights_ref[layer]).astype(BF)
        out_ref[layer, :CHUNK, 2 * RANK :] = nt(grads, weights_ref[layer, RANK:, :]).astype(BF)
        out_ref[layer, CHUNK:, :] = extra_ref[...]


def project(rows, grads, extra, weights):
    vmem = pl.BlockSpec(memory_space=pltpu.VMEM)
    return pl.pallas_call(
        project_kernel,
        out_shape=jax.ShapeDtypeStruct((LAYERS, CHUNK + EXTRA, 3 * RANK), BF),
        in_specs=[vmem] * 4,
        out_specs=vmem,
        compiler_params=pltpu.CompilerParams(vmem_limit_bytes=32 * 2**20),
        cost_estimate=pl.CostEstimate(
            flops=2 * CHUNK * SLICE * 3 * RANK * LAYERS, bytes_accessed=6 * 2**20, transcendentals=0
        ),
    )(rows, grads, extra, weights)


def block_place(low, high):
    if high - low < REACH:
        return (low, high - low)
    return (high, LAYERS - (high - low))


def chain_kernel(
    gram_hbm,
    proj_ref,
    square_ref,
    weights_ref,
    rows_ref,
    grads_ref,
    out_ref,
    gram,
    hidden,
    back,
    pre_saved,
    leave_saved,
    rows_saved,
    inv_saved,
    sems,
):
    def fetch(layer):
        for low in range(layer + 1):
            place, reach = block_place(low, layer)
            for half in range(2):
                pltpu.make_async_copy(
                    gram_hbm.at[place, 2 * reach + half],
                    gram.at[
                        pl.ds(low * RANK, RANK), pl.ds((2 * layer + half) * RANK, RANK)
                    ],
                    sems.at[layer],
                ).start()

    def arrived(layer):
        view = gram.at[pl.ds(0, (layer + 1) * RANK), pl.ds(2 * layer * RANK, 2 * RANK)]
        pltpu.make_async_copy(view, view, sems.at[layer]).wait()

    for layer in range(LAYERS):
        fetch(layer)

    square = square_ref[...]
    wide = rows_ref[...].astype(F32)
    for layer in range(LAYERS):
        arrived(layer)
        lanes = slice(2 * layer * RANK, 2 * (layer + 1) * RANK)
        total = proj_ref[layer, :CHUNK, : 2 * RANK].astype(F32)
        if layer > 1:
            before = (layer - 1) * RANK
            total = total + nn(hidden[:, :before], gram[:before, lanes])
        if layer > 0:
            near = slice((layer - 1) * RANK, layer * RANK)
            total = total + nn(hidden[:, near], gram[near, lanes])
        inverse = lax.rsqrt(square * (1.0 / WIDTH) + eps_norm)
        pre_act = total[:, :RANK] * inverse
        act = (pre_act * jax.nn.sigmoid(pre_act)).astype(BF)
        own = slice(layer * RANK, (layer + 1) * RANK)
        hidden[:, own] = act
        pre_saved[layer] = pre_act
        inv_saved[layer] = jnp.broadcast_to(inverse, (CHUNK, RANK))
        self_lanes = slice((2 * layer + 1) * RANK, 2 * (layer + 1) * RANK)
        leave_now = total[:, RANK:]
        leave_next = leave_now + nn(act, gram[own, self_lanes])
        leave_saved[layer] = leave_next
        square = jnp.maximum(
            square
            + jnp.sum(act.astype(F32) * (leave_now + leave_next), axis=1, keepdims=True),
            0.0,
        )
        rows_saved[layer] = wide.astype(BF)
        if layer < LAYERS - 1:
            wide = wide + nn(act, weights_ref[layer, RANK:, :])

    drain = jnp.zeros((CHUNK, 1), F32)
    incoming = grads_ref[...].astype(F32)
    for layer in range(LAYERS - 1, -1, -1):
        own = slice(layer * RANK, (layer + 1) * RANK)
        total = proj_ref[layer, :CHUNK, 2 * RANK :].astype(F32)
        if layer < LAYERS - 2:
            lanes = slice(2 * (layer + 2) * RANK, 2 * LAYERS * RANK)
            total = total + nt(back[:, lanes], gram[own, lanes])
        if layer < LAYERS - 1:
            near = slice(2 * (layer + 1) * RANK, 2 * (layer + 2) * RANK)
            total = total + nt(back[:, near], gram[own, near])
        pre_act = pre_saved[layer]
        inverse = inv_saved[layer]
        hidden_grad = total - drain * leave_saved[layer]
        sig_act = jax.nn.sigmoid(pre_act)
        inner = hidden_grad * (sig_act * (1.0 + pre_act * (1.0 - sig_act)))
        inner = inner.astype(BF).astype(F32)
        unit = (inner * inverse).astype(BF)
        act = hidden[:, own]
        back[:, 2 * layer * RANK : (2 * layer + 1) * RANK] = unit
        back[:, (2 * layer + 1) * RANK : (2 * layer + 2) * RANK] = (
            -drain * act.astype(F32)
        ).astype(BF)
        share = (
            jnp.sum(inner * pre_act, axis=1, keepdims=True)
            * (inverse[:, :1] * inverse[:, :1])
            * (1.0 / WIDTH)
        )
        drain = drain + share
        layer_rows = rows_saved[layer]
        out_ref[layer, :RANK, :] = tn(unit, layer_rows).astype(BF)
        out_ref[layer, RANK:, :] = tn(act, incoming.astype(BF)).astype(BF)
        if layer > 0:
            incoming = (
                incoming
                + nn(unit, weights_ref[layer, :RANK, :])
                - share * layer_rows.astype(F32)
            )


def chain(gram, proj, square, weights, rows, grads):
    vmem = pl.BlockSpec(memory_space=pltpu.VMEM)
    return pl.pallas_call(
        chain_kernel,
        out_shape=jax.ShapeDtypeStruct((LAYERS, 2 * RANK, SLICE), BF),
        in_specs=[pl.BlockSpec(memory_space=pl.ANY)] + [vmem] * 5,
        out_specs=vmem,
        scratch_shapes=[
            pltpu.VMEM((LAYERS * RANK, 2 * LAYERS * RANK), BF),
            pltpu.VMEM((CHUNK, LAYERS * RANK), BF),
            pltpu.VMEM((CHUNK, 2 * LAYERS * RANK), BF),
            pltpu.VMEM((LAYERS, CHUNK, RANK), F32),
            pltpu.VMEM((LAYERS, CHUNK, RANK), F32),
            pltpu.VMEM((LAYERS, CHUNK, SLICE), BF),
            pltpu.VMEM((LAYERS, CHUNK, RANK), F32),
            pltpu.SemaphoreType.DMA((LAYERS,)),
        ],
        compiler_params=pltpu.CompilerParams(vmem_limit_bytes=56 * 2**20),
        cost_estimate=pl.CostEstimate(
            flops=4 * 2**30, bytes_accessed=20 * 2**20, transcendentals=2**20
        ),
    )(gram, proj, square, weights, rows, grads)


def per_device(
    micro_inputs,
    cotangent,
    norm_gain,
    enter_weight,
    enter_moment,
    enter_second,
    leave_weight,
    leave_moment,
    leave_second,
):
    section = lax.axis_index(SECTION)
    part = lax.axis_index(DP)
    gain = lax.dynamic_slice_in_dim(norm_gain[0], part * SLICE, SLICE).astype(F32)

    with jax.named_scope("weights"):
        enter_half = enter_weight[0].astype(BF).astype(F32)
        scaled = (enter_half * gain[:, None]).astype(BF)
        own = jnp.concatenate([scaled.T, leave_weight[0].astype(BF)], axis=0)
        weights = lax.all_gather(own, SECTION, axis=0, tiled=False)

    with jax.named_scope("rows"):
        own_rows = CHUNK // PARTS
        both = jnp.stack(
            [
                lax.dynamic_slice_in_dim(
                    value.reshape(CHUNK, WIDTH), section * own_rows, own_rows, 0
                )
                for value in (micro_inputs, cotangent)
            ]
        )
        both = both.reshape(2 * own_rows, PARTS, SLICE).transpose(1, 0, 2)
        both = lax.all_to_all(both, DP, split_axis=0, concat_axis=0, tiled=True)
        both = both.reshape(PARTS, 2, own_rows, SLICE)
        rows = both[:, 0].reshape(CHUNK, SLICE)
        grads = both[:, 1].reshape(CHUNK, SLICE)

    with jax.named_scope("gram"):
        blocks = gram_blocks(section, weights)
        pieces = blocks.reshape(PARTS, 2 * REACH * RANK // PARTS, RANK)
        pieces = lax.all_to_all(pieces, DP, split_axis=0, concat_axis=0, tiled=True)
        piece = jnp.sum(pieces.astype(F32), axis=0).astype(BF)
        spread = jnp.broadcast_to(piece[None], pieces.shape)
        blocks = lax.all_to_all(spread, DP, split_axis=0, concat_axis=0, tiled=True)
        blocks = blocks.reshape(2 * REACH, RANK, RANK)
        gram = lax.all_gather(blocks, SECTION, axis=0, tiled=False)

    with jax.named_scope("project"):
        wide = rows.astype(F32)
        square = jnp.sum(wide * wide, axis=1)
        high = square.astype(BF)
        low = (square - high.astype(F32)).astype(BF)
        extra = jnp.zeros((EXTRA, 3 * RANK), BF)
        extra = extra.at[0, :CHUNK].set(high).at[1, :CHUNK].set(low)
        proj = project(rows, grads, extra, weights)
        proj = lax.all_to_all(proj, DP, split_axis=0, concat_axis=0, tiled=True)
        proj = jnp.sum(proj.astype(F32), axis=0)
        square = proj[CHUNK, :CHUNK] + proj[CHUNK + 1, :CHUNK]
        proj = jnp.broadcast_to(proj.astype(BF)[None], (PARTS,) + proj.shape)
        proj = lax.all_to_all(proj, DP, split_axis=0, concat_axis=0, tiled=True)

    with jax.named_scope("chain"):
        shares = chain(gram, proj, square[:, None], weights, rows, grads)

    with jax.named_scope("sum"):
        shares = lax.all_to_all(shares, SECTION, split_axis=0, concat_axis=0, tiled=True)
        total = jnp.sum(shares.astype(F32), axis=0)

    with jax.named_scope("adam"):
        enter_grad = total[:RANK].T * gain[:, None]
        leave_grad = total[RANK:]
        new_enter = adam_update(enter_weight[0], enter_moment[0], enter_second[0], enter_grad)
        new_leave = adam_update(leave_weight[0], leave_moment[0], leave_second[0], leave_grad)
    return tuple(value[None] for value in new_enter + new_leave)


def solution(mesh):
    split = Mesh(mesh.devices.reshape(2, 4, 2, 2, 8), SECTION + DP)
    rows = P(None, None, DP, None)
    enter = P(SECTION, DP, None)
    leave = P(SECTION, None, DP)
    return jax.shard_map(
        per_device,
        mesh=split,
        in_specs=(rows, rows, P(SECTION, None)) + (enter,) * 3 + (leave,) * 3,
        out_specs=(enter,) * 3 + (leave,) * 3,
        check_vma=False,
    )
```

```python
import jax
import jax.numpy as jnp
from jax import lax
from jax.experimental import pallas as pl
from jax.experimental.pallas import tpu as pltpu
from jax.sharding import Mesh, PartitionSpec as P

eps_norm = 1e-05
rate = 0.001
beta_one = 0.9
beta_two = 0.95
adam_eps = 1e-08
step_count = 10

LAYERS = 16
RANK = 128
WIDTH = 8192
PARTS = 16
SLICE = WIDTH // PARTS
CHUNK = 128
OWN_ROWS = CHUNK // PARTS
HALF = LAYERS // 2
PACKED = RANK + 4 * 2 * OWN_ROWS + 2 * OWN_ROWS

SECTION = ("xh", "y", "c")
DP = ("xl", "z")

BF = jnp.bfloat16
F32 = jnp.float32


def nn(a, b):
    return lax.dot_general(a, b, (((1,), (0,)), ((), ())), preferred_element_type=F32)


def nt(a, b):
    return lax.dot_general(a, b, (((1,), (1,)), ((), ())), preferred_element_type=F32)


def tn(a, b):
    return lax.dot_general(a, b, (((0,), (0,)), ((), ())), preferred_element_type=F32)


VMEM = pl.BlockSpec(memory_space=pltpu.VMEM)
SMEM = pl.BlockSpec(memory_space=pltpu.SMEM)
ANY = pl.BlockSpec(memory_space=pl.ANY)


def params(mebibytes):
    return pltpu.CompilerParams(vmem_limit_bytes=mebibytes * 2**20)


def cost(flops, bytes_accessed):
    return pl.CostEstimate(flops=flops, bytes_accessed=bytes_accessed, transcendentals=0)


def own_kernel(enter_ref, leave_ref, gain_ref, out_ref):
    enter = enter_ref[0].astype(BF).astype(F32).T * gain_ref[...]
    enter = enter.astype(BF)
    leave = leave_ref[0].astype(BF)
    for copy in range(HALF):
        out_ref[copy, :RANK, :] = enter
        out_ref[copy, RANK:, :] = leave


def own_weights(enter_weight, leave_weight, gain):
    return pl.pallas_call(
        own_kernel,
        out_shape=jax.ShapeDtypeStruct((HALF, 2 * RANK, SLICE), BF),
        in_specs=[VMEM] * 3,
        out_specs=VMEM,
        compiler_params=params(16),
        cost_estimate=cost(2**18, 3 * 2**20),
    )(enter_weight, leave_weight, gain)


def load_weights(core, near_ref, far_ref, weights, sems):
    copies = [
        pltpu.make_async_copy(near_ref, weights.at[core], sems.at[0]),
        pltpu.make_async_copy(far_ref, weights.at[1 - core], sems.at[1]),
    ]
    for copy in copies:
        copy.start()
    return copies


def gram_kernel(index_ref, near_ref, far_ref, both_ref, out_ref, weights, sems):
    section = index_ref[0]
    copies = load_weights(index_ref[1], near_ref, far_ref, weights, sems)
    both = both_ref[...]
    for part in range(PARTS):
        for lane in range(SLICE // 128):
            first = RANK + 2 * OWN_ROWS * lane
            start = SLICE * part + 128 * lane
            out_ref[part, first : first + 2 * OWN_ROWS, :] = both[:, start : start + 128]
    wide = both.astype(F32)[:OWN_ROWS]
    square = jnp.sum(wide * wide, axis=1, keepdims=True)
    high = square.astype(BF).astype(F32)
    tail = jnp.concatenate(
        [
            jnp.broadcast_to(high, (OWN_ROWS, RANK)),
            jnp.broadcast_to(square - high, (OWN_ROWS, RANK)),
        ],
        axis=0,
    ).astype(BF)
    for part in range(PARTS):
        out_ref[part, PACKED - 2 * OWN_ROWS :, :] = tail
    for copy in copies:
        copy.wait()

    def layer_rows(layer, rows):
        return weights[lax.rem(layer, 2), layer // 2, rows, :]

    leave = pl.ds(RANK, RANK)
    out_ref[0, :RANK, :] = nt(layer_rows(section, leave), layer_rows(section, leave)).astype(BF)
    for reach in range(1, HALF + 1):
        other = lax.rem(section + reach, LAYERS)
        low = jnp.minimum(section, other)
        high = jnp.maximum(section, other)
        if reach < HALF:
            block = nt(layer_rows(low, leave), layer_rows(high, pl.ds(0, 2 * RANK))).astype(BF)
            out_ref[2 * reach - 1, :RANK, :] = block[:, :RANK]
            out_ref[2 * reach, :RANK, :] = block[:, RANK:]
        else:
            start = pl.multiple_of((section // HALF) * RANK, RANK)
            block = nt(layer_rows(low, leave), layer_rows(high, pl.ds(start, RANK)))
            out_ref[2 * reach - 1, :RANK, :] = block.astype(BF)


def gram_and_rows(index, near, far, both):
    return pl.pallas_call(
        gram_kernel,
        out_shape=jax.ShapeDtypeStruct((PARTS, PACKED, RANK), BF),
        in_specs=[SMEM, ANY, ANY, VMEM],
        out_specs=VMEM,
        scratch_shapes=[
            pltpu.VMEM((2, HALF, 2 * RANK, SLICE), BF),
            pltpu.SemaphoreType.DMA((2,)),
        ],
        compiler_params=params(32),
        cost_estimate=cost(2 * LAYERS * RANK * RANK * SLICE, 6 * 2**20),
    )(index, near, far, both)


def block_place(low, high, half):
    reach = high - low
    if reach == 0:
        return (low, 0)
    if reach < HALF:
        return (low, 2 * reach - 1 + half)
    if reach == HALF:
        return ((low, high)[half], LAYERS - 1)
    return (high, 2 * (LAYERS - reach) - 1 + half)


def project_kernel(
    index_ref, packed_ref, near_ref, far_ref, out_ref, rows_ref, grads_ref, square_ref, weights, sems
):
    copies = load_weights(index_ref[1], near_ref, far_ref, weights, sems)
    lanes = []
    for lane in range(SLICE // 128):
        first = RANK + 2 * OWN_ROWS * lane
        lanes.append(packed_ref[:, first : first + 2 * OWN_ROWS, :].astype(F32))
    both = jnp.concatenate(lanes, axis=2)
    rows = both[:, :OWN_ROWS, :].reshape(CHUNK, SLICE).astype(BF)
    grads = both[:, OWN_ROWS:, :].reshape(CHUNK, SLICE).astype(BF)
    rows_ref[...] = rows
    grads_ref[...] = grads
    tail = packed_ref[:, PACKED - 2 * OWN_ROWS :, :].astype(F32)
    square_ref[...] = (tail[:, :OWN_ROWS, :] + tail[:, OWN_ROWS:, :]).reshape(CHUNK, RANK)
    for copy in copies:
        copy.wait()
    for layer in range(LAYERS):
        place = (layer % 2, layer // 2)
        out_ref[layer, :, : 2 * RANK] = nt(rows, weights[place]).astype(BF)
        out_ref[layer, :, 2 * RANK :] = nt(grads, weights[place][RANK:, :]).astype(BF)


def project(index, packed, near, far):
    return pl.pallas_call(
        project_kernel,
        out_shape=(
            jax.ShapeDtypeStruct((LAYERS, CHUNK, 3 * RANK), BF),
            jax.ShapeDtypeStruct((CHUNK, SLICE), BF),
            jax.ShapeDtypeStruct((CHUNK, SLICE), BF),
            jax.ShapeDtypeStruct((CHUNK, RANK), F32),
        ),
        in_specs=[SMEM, VMEM, ANY, ANY],
        out_specs=(VMEM,) * 4,
        scratch_shapes=[
            pltpu.VMEM((2, HALF, 2 * RANK, SLICE), BF),
            pltpu.SemaphoreType.DMA((2,)),
        ],
        compiler_params=params(32),
        cost_estimate=cost(2 * CHUNK * SLICE * 3 * RANK * LAYERS, 7 * 2**20),
    )(index, packed, near, far)


def chain_kernel(
    index_ref,
    gram_hbm,
    proj_ref,
    square_ref,
    near_ref,
    far_ref,
    rows_ref,
    grads_ref,
    keep_ref,
    pass_ref,
    gram,
    weights,
    shares,
    hidden,
    back,
    pre_saved,
    leave_saved,
    rows_saved,
    inv_saved,
    gram_sems,
    sems,
    out_sems,
):
    core = index_ref[1]
    copies = load_weights(core, near_ref, far_ref, weights, sems)

    def fetch(layer):
        for low in range(layer + 1):
            for half in range(2):
                if low == layer and half == 0:
                    continue
                place, slot = block_place(low, layer, half)
                pltpu.make_async_copy(
                    gram_hbm.at[place, slot],
                    gram.at[
                        pl.ds(low * RANK, RANK), pl.ds((2 * layer + half) * RANK, RANK)
                    ],
                    gram_sems.at[layer],
                ).start()

    def arrived(layer):
        view = gram.at[pl.ds(0, (2 * layer + 1) * (RANK // 2)), pl.ds(0, 2 * RANK)]
        pltpu.make_async_copy(view, view, gram_sems.at[layer]).wait()

    for layer in range(LAYERS):
        fetch(layer)
    for copy in copies:
        copy.wait()

    square = square_ref[...][:, :1]
    wide = rows_ref[...].astype(F32)
    for layer in range(LAYERS):
        arrived(layer)
        lanes = slice(2 * layer * RANK, 2 * (layer + 1) * RANK)
        total = proj_ref[layer, :, : 2 * RANK].astype(F32)
        if layer > 1:
            before = (layer - 1) * RANK
            total = total + nn(hidden[:, :before], gram[:before, lanes])
        if layer > 0:
            near = slice((layer - 1) * RANK, layer * RANK)
            total = total + nn(hidden[:, near], gram[near, lanes])
        inverse = lax.rsqrt(square * (1.0 / WIDTH) + eps_norm)
        pre_act = total[:, :RANK] * inverse
        act = (pre_act * jax.nn.sigmoid(pre_act)).astype(BF)
        own = slice(layer * RANK, (layer + 1) * RANK)
        hidden[:, own] = act
        pre_saved[layer] = pre_act
        inv_saved[layer] = jnp.broadcast_to(inverse, (CHUNK, RANK))
        self_lanes = slice((2 * layer + 1) * RANK, 2 * (layer + 1) * RANK)
        leave_now = total[:, RANK:]
        leave_next = leave_now + nn(act, gram[own, self_lanes])
        leave_saved[layer] = leave_next
        square = jnp.maximum(
            square
            + jnp.sum(act.astype(F32) * (leave_now + leave_next), axis=1, keepdims=True),
            0.0,
        )
        rows_saved[layer] = wide.astype(BF)
        if layer < LAYERS - 1:
            wide = wide + nn(act, weights[layer % 2, layer // 2, RANK:, :])

    drain = jnp.zeros((CHUNK, 1), F32)
    incoming = grads_ref[...].astype(F32)
    for layer in range(LAYERS - 1, -1, -1):
        own = slice(layer * RANK, (layer + 1) * RANK)
        total = proj_ref[layer, :, 2 * RANK :].astype(F32)
        if layer < LAYERS - 2:
            lanes = slice(2 * (layer + 2) * RANK, 2 * LAYERS * RANK)
            total = total + nt(back[:, lanes], gram[own, lanes])
        if layer < LAYERS - 1:
            near = slice(2 * (layer + 1) * RANK, 2 * (layer + 2) * RANK)
            total = total + nt(back[:, near], gram[own, near])
        pre_act = pre_saved[layer]
        inverse = inv_saved[layer]
        hidden_grad = total - drain * leave_saved[layer]
        sig_act = jax.nn.sigmoid(pre_act)
        inner = hidden_grad * (sig_act * (1.0 + pre_act * (1.0 - sig_act)))
        inner = inner.astype(BF).astype(F32)
        unit = (inner * inverse).astype(BF)
        act = hidden[:, own]
        back[:, 2 * layer * RANK : (2 * layer + 1) * RANK] = unit
        back[:, (2 * layer + 1) * RANK : (2 * layer + 2) * RANK] = (
            -drain * act.astype(F32)
        ).astype(BF)
        share = (
            jnp.sum(inner * pre_act, axis=1, keepdims=True)
            * (inverse[:, :1] * inverse[:, :1])
            * (1.0 / WIDTH)
        )
        drain = drain + share
        layer_rows = rows_saved[layer]
        side = core if layer % 2 == 0 else 1 - core
        shares[side, layer // 2, :RANK, :] = tn(unit, layer_rows).astype(BF)
        shares[side, layer // 2, RANK:, :] = tn(act, incoming.astype(BF)).astype(BF)
        if layer > 0:
            incoming = (
                incoming
                + nn(unit, weights[layer % 2, layer // 2, :RANK, :])
                - share * layer_rows.astype(F32)
            )
    last = [
        pltpu.make_async_copy(shares.at[0], keep_ref, out_sems.at[0]),
        pltpu.make_async_copy(shares.at[1], pass_ref, out_sems.at[1]),
    ]
    for copy in last:
        copy.start()
    for copy in last:
        copy.wait()


def chain(index, gram, proj, square, near, far, rows, grads):
    side = jax.ShapeDtypeStruct((HALF, 2 * RANK, SLICE), BF)
    return pl.pallas_call(
        chain_kernel,
        out_shape=(side, side),
        in_specs=[SMEM, ANY, VMEM, VMEM, ANY, ANY, VMEM, VMEM],
        out_specs=(ANY, ANY),
        scratch_shapes=[
            pltpu.VMEM((LAYERS * RANK, 2 * LAYERS * RANK), BF),
            pltpu.VMEM((2, HALF, 2 * RANK, SLICE), BF),
            pltpu.VMEM((2, HALF, 2 * RANK, SLICE), BF),
            pltpu.VMEM((CHUNK, LAYERS * RANK), BF),
            pltpu.VMEM((CHUNK, 2 * LAYERS * RANK), BF),
            pltpu.VMEM((LAYERS, CHUNK, RANK), F32),
            pltpu.VMEM((LAYERS, CHUNK, RANK), F32),
            pltpu.VMEM((LAYERS, CHUNK, SLICE), BF),
            pltpu.VMEM((LAYERS, CHUNK, RANK), F32),
            pltpu.SemaphoreType.DMA((LAYERS,)),
            pltpu.SemaphoreType.DMA((2,)),
            pltpu.SemaphoreType.DMA((2,)),
        ],
        compiler_params=params(56),
        cost_estimate=cost(4 * 2**30, 20 * 2**20),
    )(index, gram, proj, square, near, far, rows, grads)


def adam_update(weight, moment, second, grad):
    moment_new = beta_one * moment + (1.0 - beta_one) * grad
    second_new = beta_two * second + (1.0 - beta_two) * grad * grad
    corr_one = 1.0 - beta_one**step_count
    corr_two = 1.0 - beta_two**step_count
    weight_new = weight - rate * (moment_new / corr_one) / (
        jnp.sqrt(second_new / corr_two) + adam_eps
    )
    return (weight_new, moment_new, second_new)


def adam_kernel(parts_ref, gain_ref, *refs):
    ins, outs = refs[:6], refs[6:]
    total = jnp.sum(parts_ref[...].astype(F32), axis=0)
    grads = ((total[:RANK] * gain_ref[...]).T, total[RANK:])
    for first, grad in zip((0, 3), grads):
        updated = adam_update(*(ref[0] for ref in ins[first : first + 3]), grad)
        for ref, value in zip(outs[first : first + 3], updated):
            ref[0] = value


def adam(parts, gain, state):
    return pl.pallas_call(
        adam_kernel,
        out_shape=tuple(jax.ShapeDtypeStruct(value.shape, F32) for value in state),
        in_specs=[VMEM] * 8,
        out_specs=(VMEM,) * 6,
        compiler_params=params(32),
        cost_estimate=cost(2**22, 5 * 2**20),
    )(parts, gain, *state)


def per_device(
    micro_inputs,
    cotangent,
    norm_gain,
    enter_weight,
    enter_moment,
    enter_second,
    leave_weight,
    leave_moment,
    leave_second,
):
    section = lax.axis_index(SECTION)
    part = lax.axis_index(DP)
    core = lax.axis_index("c")
    index = jnp.stack([section, core])
    gain = lax.dynamic_slice_in_dim(norm_gain, part * SLICE, SLICE, axis=1).astype(F32)
    cores = [(0, 1), (1, 0)]

    def exchange(value, axes):
        return lax.all_to_all(value, axes, split_axis=0, concat_axis=0, tiled=True)

    def spread(value):
        return exchange(jnp.broadcast_to(value[None], (PARTS,) + value.shape), DP)

    with jax.named_scope("weights"):
        near = exchange(own_weights(enter_weight, leave_weight, gain), ("xh", "y"))
        far = lax.ppermute(near, "c", cores)

    with jax.named_scope("gram"):
        both = jnp.concatenate(
            [
                lax.dynamic_slice_in_dim(
                    value.reshape(CHUNK, WIDTH), section * OWN_ROWS, OWN_ROWS, 0
                )
                for value in (micro_inputs, cotangent)
            ]
        )
        packed = exchange(gram_and_rows(index, near, far, both), DP)
        blocks = spread(jnp.sum(packed[:, :RANK, :].astype(F32), axis=0).astype(BF))
        gram = lax.all_gather(blocks, SECTION, axis=0, tiled=False)

    with jax.named_scope("project"):
        proj, rows, grads, square = project(index, packed, near, far)
        proj = spread(jnp.sum(exchange(proj, DP).astype(F32), axis=0).astype(BF))

    with jax.named_scope("chain"):
        keep, other = chain(index, gram, proj, square, near, far, rows, grads)

    with jax.named_scope("sum"):
        received = lax.ppermute(other, "c", cores)
        parts = exchange((keep.astype(F32) + received.astype(F32)).astype(BF), ("xh", "y"))

    with jax.named_scope("adam"):
        return adam(
            parts,
            gain,
            (enter_weight, enter_moment, enter_second, leave_weight, leave_moment, leave_second),
        )


def solution(mesh):
    split = Mesh(mesh.devices.reshape(2, 4, 2, 2, 8), SECTION + DP)
    rows = P(None, None, DP, None)
    enter = P(SECTION, DP, None)
    leave = P(SECTION, None, DP)
    return jax.shard_map(
        per_device,
        mesh=split,
        in_specs=(rows, rows, P(SECTION, None)) + (enter,) * 3 + (leave,) * 3,
        out_specs=(enter,) * 3 + (leave,) * 3,
        check_vma=False,
    )
```

```python
import jax
import jax.numpy as jnp
from jax import lax
from jax.experimental import pallas as pl
from jax.experimental.pallas import tpu as pltpu
from jax.sharding import Mesh, PartitionSpec as P

eps_norm = 1e-05
rate = 0.001
beta_one = 0.9
beta_two = 0.95
adam_eps = 1e-08
step_count = 10

LAYERS = 16
RANK = 128
WIDTH = 8192
PARTS = 16
SLICE = WIDTH // PARTS
CHUNK = 128
OWN_ROWS = CHUNK // PARTS
HALF = LAYERS // 2
PIECE = HALF * RANK // PARTS
LANES = 2 * RANK
SPANS = SLICE // LANES
TAIL = PIECE + SPANS * 2 * OWN_ROWS
PACKED = TAIL + 2 * OWN_ROWS

SECTION = ("xh", "y", "c")
DP = ("xl", "z")

BF = jnp.bfloat16
F32 = jnp.float32


def nn(a, b):
    return lax.dot_general(a, b, (((1,), (0,)), ((), ())), preferred_element_type=F32)


def nt(a, b):
    return lax.dot_general(a, b, (((1,), (1,)), ((), ())), preferred_element_type=F32)


def tn(a, b):
    return lax.dot_general(a, b, (((0,), (0,)), ((), ())), preferred_element_type=F32)


VMEM = pl.BlockSpec(memory_space=pltpu.VMEM)
SMEM = pl.BlockSpec(memory_space=pltpu.SMEM)
ANY = pl.BlockSpec(memory_space=pl.ANY)


def params(mebibytes):
    return pltpu.CompilerParams(vmem_limit_bytes=mebibytes * 2**20)


def cost(flops, bytes_accessed):
    return pl.CostEstimate(flops=flops, bytes_accessed=bytes_accessed, transcendentals=0)


def own_kernel(enter_ref, leave_ref, gain_ref, out_ref):
    enter = enter_ref[0].astype(BF).astype(F32).T * gain_ref[...]
    enter = enter.astype(BF)
    leave = leave_ref[0].astype(BF)
    for copy in range(HALF):
        out_ref[copy, :RANK, :] = enter
        out_ref[copy, RANK:, :] = leave


def own_weights(enter_weight, leave_weight, gain):
    return pl.pallas_call(
        own_kernel,
        out_shape=jax.ShapeDtypeStruct((HALF, 2 * RANK, SLICE), BF),
        in_specs=[VMEM] * 3,
        out_specs=VMEM,
        compiler_params=params(16),
        cost_estimate=cost(2**18, 3 * 2**20),
    )(enter_weight, leave_weight, gain)


def load_weights(core, near_ref, far_ref, weights, sems):
    copies = [
        pltpu.make_async_copy(near_ref, weights.at[core], sems.at[0]),
        pltpu.make_async_copy(far_ref, weights.at[1 - core], sems.at[1]),
    ]
    for copy in copies:
        copy.start()
    return copies


def gram_kernel(index_ref, near_ref, far_ref, both_ref, out_ref, weights, sems):
    section = index_ref[0]
    copies = load_weights(index_ref[1], near_ref, far_ref, weights, sems)
    both = both_ref[...]
    for part in range(PARTS):
        for span in range(SPANS):
            first = PIECE + 2 * OWN_ROWS * span
            start = SLICE * part + LANES * span
            out_ref[part, first : first + 2 * OWN_ROWS, :] = both[:, start : start + LANES]
    wide = both.astype(F32)[:OWN_ROWS]
    square = jnp.sum(wide * wide, axis=1, keepdims=True)
    high = square.astype(BF).astype(F32)
    tail = jnp.concatenate(
        [
            jnp.broadcast_to(high, (OWN_ROWS, LANES)),
            jnp.broadcast_to(square - high, (OWN_ROWS, LANES)),
        ],
        axis=0,
    ).astype(BF)
    for part in range(PARTS):
        out_ref[part, TAIL:, :] = tail
    for copy in copies:
        copy.wait()

    def layer_rows(layer, rows):
        return weights[lax.rem(layer, 2), layer // 2, rows, :]

    leave = pl.ds(RANK, RANK)
    for reach in range(HALF):
        other = lax.rem(section + reach, LAYERS)
        low = layer_rows(jnp.minimum(section, other), leave)
        if reach > 0:
            block = nt(low, layer_rows(jnp.maximum(section, other), pl.ds(0, 2 * RANK)))
        else:
            across = lax.rem(section + HALF, LAYERS)
            start = pl.multiple_of((section // HALF) * RANK, RANK)
            far_rows = layer_rows(jnp.maximum(section, across), pl.ds(start, RANK))
            near_rows = layer_rows(jnp.minimum(section, across), leave)
            block = jnp.concatenate([nt(near_rows, far_rows), nt(low, low)], axis=1)
        block = block.astype(BF)
        out_ref[2 * reach, :PIECE, :] = block[:PIECE]
        out_ref[2 * reach + 1, :PIECE, :] = block[PIECE:]


def gram_and_rows(index, near, far, both):
    return pl.pallas_call(
        gram_kernel,
        out_shape=jax.ShapeDtypeStruct((PARTS, PACKED, LANES), BF),
        in_specs=[SMEM, ANY, ANY, VMEM],
        out_specs=VMEM,
        scratch_shapes=[
            pltpu.VMEM((2, HALF, 2 * RANK, SLICE), BF),
            pltpu.SemaphoreType.DMA((2,)),
        ],
        compiler_params=params(32),
        cost_estimate=cost(2 * LAYERS * RANK * RANK * SLICE, 6 * 2**20),
    )(index, near, far, both)


def project_kernel(
    index_ref, packed_ref, near_ref, far_ref, out_ref, rows_ref, grads_ref, square_ref, weights, sems
):
    copies = load_weights(index_ref[1], near_ref, far_ref, weights, sems)
    lanes = []
    for span in range(SPANS):
        first = PIECE + 2 * OWN_ROWS * span
        lanes.append(packed_ref[:, first : first + 2 * OWN_ROWS, :].astype(F32))
    both = jnp.concatenate(lanes, axis=2)
    rows = both[:, :OWN_ROWS, :].reshape(CHUNK, SLICE).astype(BF)
    grads = both[:, OWN_ROWS:, :].reshape(CHUNK, SLICE).astype(BF)
    rows_ref[...] = rows
    grads_ref[...] = grads
    tail = packed_ref[:, TAIL:, :RANK].astype(F32)
    square_ref[...] = (tail[:, :OWN_ROWS, :] + tail[:, OWN_ROWS:, :]).reshape(CHUNK, RANK)
    for copy in copies:
        copy.wait()
    for layer in range(LAYERS):
        place = (layer % 2, layer // 2)
        out_ref[layer, :, : 2 * RANK] = nt(rows, weights[place]).astype(BF)
        out_ref[layer, :, 2 * RANK :] = nt(grads, weights[place][RANK:, :]).astype(BF)


def project(index, packed, near, far):
    return pl.pallas_call(
        project_kernel,
        out_shape=(
            jax.ShapeDtypeStruct((LAYERS, CHUNK, 3 * RANK), BF),
            jax.ShapeDtypeStruct((CHUNK, SLICE), BF),
            jax.ShapeDtypeStruct((CHUNK, SLICE), BF),
            jax.ShapeDtypeStruct((CHUNK, RANK), F32),
        ),
        in_specs=[SMEM, VMEM, ANY, ANY],
        out_specs=(VMEM,) * 4,
        scratch_shapes=[
            pltpu.VMEM((2, HALF, 2 * RANK, SLICE), BF),
            pltpu.SemaphoreType.DMA((2,)),
        ],
        compiler_params=params(32),
        cost_estimate=cost(2 * CHUNK * SLICE * 3 * RANK * LAYERS, 7 * 2**20),
    )(index, packed, near, far)


def chain_kernel(
    index_ref,
    *refs,
):
    block_refs = refs[:LAYERS]
    (
        proj_ref,
        square_ref,
        near_ref,
        far_ref,
        rows_ref,
        grads_ref,
        keep_ref,
        pass_ref,
        gram,
        weights,
        shares,
        hidden,
        back,
        pre_saved,
        leave_saved,
        rows_saved,
        inv_saved,
        gram_sems,
        sems,
        out_sems,
    ) = refs[LAYERS:]
    core = index_ref[1]
    copies = load_weights(core, near_ref, far_ref, weights, sems)

    plane, ring = index_ref[2], index_ref[3]

    def place(ref, low, high, lane, width):
        rows = pl.ds(pl.multiple_of(low * RANK, RANK), RANK)
        first = pl.multiple_of((2 * high + lane) * RANK, RANK)
        pltpu.make_async_copy(
            ref, gram.at[rows, pl.ds(first, width)], gram_sems.at[high]
        ).start()

    def fetch(block_ref, step_plane, step_ring, step_core):
        across_plane = plane if step_plane == 0 else 1 - plane
        across_core = core if step_core == 0 else 1 - core
        layer = (across_plane * 4 + lax.rem(ring + step_ring, 4)) * 2 + across_core
        place(block_ref.at[0, :, pl.ds(RANK, RANK)], layer, layer, 1, RANK)
        for reach in range(1, HALF):
            other = lax.rem(layer + reach, LAYERS)
            low, high = jnp.minimum(layer, other), jnp.maximum(layer, other)
            place(block_ref.at[reach], low, high, 0, 2 * RANK)
        other = lax.rem(layer + HALF, LAYERS)
        low, high = jnp.minimum(layer, other), jnp.maximum(layer, other)
        place(block_ref.at[0, :, pl.ds(0, RANK)], low, high, layer // HALF, RANK)

    steps = [(core, plane, ring) for core in (0, 1) for plane in (0, 1) for ring in range(4)]
    for (step_core, step_plane, step_ring), block_ref in zip(steps, block_refs):
        fetch(block_ref, step_plane, step_ring, step_core)

    def arrived(layer):
        view = gram.at[pl.ds(0, (2 * layer + 1) * (RANK // 2)), pl.ds(0, 2 * RANK)]
        pltpu.make_async_copy(view, view, gram_sems.at[layer]).wait()

    square = square_ref[...][:, :1]
    wide = rows_ref[...].astype(F32)
    for layer in range(LAYERS):
        arrived(layer)
        lanes = slice(2 * layer * RANK, 2 * (layer + 1) * RANK)
        total = proj_ref[layer, :, : 2 * RANK].astype(F32)
        if layer > 1:
            before = (layer - 1) * RANK
            total = total + nn(hidden[:, :before], gram[:before, lanes])
        if layer > 0:
            near = slice((layer - 1) * RANK, layer * RANK)
            total = total + nn(hidden[:, near], gram[near, lanes])
        inverse = lax.rsqrt(square * (1.0 / WIDTH) + eps_norm)
        pre_act = total[:, :RANK] * inverse
        act = (pre_act * jax.nn.sigmoid(pre_act)).astype(BF)
        own = slice(layer * RANK, (layer + 1) * RANK)
        hidden[:, own] = act
        pre_saved[layer] = pre_act
        inv_saved[layer] = jnp.broadcast_to(inverse, (CHUNK, RANK))
        self_lanes = slice((2 * layer + 1) * RANK, 2 * (layer + 1) * RANK)
        leave_now = total[:, RANK:]
        leave_next = leave_now + nn(act, gram[own, self_lanes])
        leave_saved[layer] = leave_next
        square = jnp.maximum(
            square
            + jnp.sum(act.astype(F32) * (leave_now + leave_next), axis=1, keepdims=True),
            0.0,
        )
        rows_saved[layer] = wide.astype(BF)
        if layer == 0:
            for copy in copies:
                copy.wait()
        if layer < LAYERS - 1:
            wide = wide + nn(act, weights[layer % 2, layer // 2, RANK:, :])

    drain = jnp.zeros((CHUNK, 1), F32)
    incoming = grads_ref[...].astype(F32)
    for layer in range(LAYERS - 1, -1, -1):
        own = slice(layer * RANK, (layer + 1) * RANK)
        total = proj_ref[layer, :, 2 * RANK :].astype(F32)
        if layer < LAYERS - 2:
            lanes = slice(2 * (layer + 2) * RANK, 2 * LAYERS * RANK)
            total = total + nt(back[:, lanes], gram[own, lanes])
        if layer < LAYERS - 1:
            near = slice(2 * (layer + 1) * RANK, 2 * (layer + 2) * RANK)
            total = total + nt(back[:, near], gram[own, near])
        pre_act = pre_saved[layer]
        inverse = inv_saved[layer]
        hidden_grad = total - drain * leave_saved[layer]
        sig_act = jax.nn.sigmoid(pre_act)
        inner = hidden_grad * (sig_act * (1.0 + pre_act * (1.0 - sig_act)))
        inner = inner.astype(BF).astype(F32)
        unit = (inner * inverse).astype(BF)
        act = hidden[:, own]
        back[:, 2 * layer * RANK : (2 * layer + 1) * RANK] = unit
        back[:, (2 * layer + 1) * RANK : (2 * layer + 2) * RANK] = (
            -drain * act.astype(F32)
        ).astype(BF)
        share = (
            jnp.sum(inner * pre_act, axis=1, keepdims=True)
            * (inverse[:, :1] * inverse[:, :1])
            * (1.0 / WIDTH)
        )
        drain = drain + share
        layer_rows = rows_saved[layer]
        side = core if layer % 2 == 0 else 1 - core
        shares[side, layer // 2, :RANK, :] = tn(unit, layer_rows).astype(BF)
        shares[side, layer // 2, RANK:, :] = tn(act, incoming.astype(BF)).astype(BF)
        if layer > 0:
            incoming = (
                incoming
                + nn(unit, weights[layer % 2, layer // 2, :RANK, :])
                - share * layer_rows.astype(F32)
            )
    last = [
        pltpu.make_async_copy(shares.at[0], keep_ref, out_sems.at[0]),
        pltpu.make_async_copy(shares.at[1], pass_ref, out_sems.at[1]),
    ]
    for copy in last:
        copy.start()
    for copy in last:
        copy.wait()


def chain(index, gram, proj, square, near, far, rows, grads):
    side = jax.ShapeDtypeStruct((HALF, 2 * RANK, SLICE), BF)
    return pl.pallas_call(
        chain_kernel,
        out_shape=(side, side),
        in_specs=[SMEM] + [ANY] * LAYERS + [VMEM, VMEM, ANY, ANY, VMEM, VMEM],
        out_specs=(ANY, ANY),
        scratch_shapes=[
            pltpu.VMEM((LAYERS * RANK, 2 * LAYERS * RANK), BF),
            pltpu.VMEM((2, HALF, 2 * RANK, SLICE), BF),
            pltpu.VMEM((2, HALF, 2 * RANK, SLICE), BF),
            pltpu.VMEM((CHUNK, LAYERS * RANK), BF),
            pltpu.VMEM((CHUNK, 2 * LAYERS * RANK), BF),
            pltpu.VMEM((LAYERS, CHUNK, RANK), F32),
            pltpu.VMEM((LAYERS, CHUNK, RANK), F32),
            pltpu.VMEM((LAYERS, CHUNK, SLICE), BF),
            pltpu.VMEM((LAYERS, CHUNK, RANK), F32),
            pltpu.SemaphoreType.DMA((LAYERS,)),
            pltpu.SemaphoreType.DMA((2,)),
            pltpu.SemaphoreType.DMA((2,)),
        ],
        compiler_params=params(56),
        cost_estimate=cost(4 * 2**30, 20 * 2**20),
    )(index, *gram, proj, square, near, far, rows, grads)


def adam_update(weight, moment, second, grad):
    moment_new = beta_one * moment + (1.0 - beta_one) * grad
    second_new = beta_two * second + (1.0 - beta_two) * grad * grad
    corr_one = 1.0 - beta_one**step_count
    corr_two = 1.0 - beta_two**step_count
    weight_new = weight - rate * (moment_new / corr_one) / (
        jnp.sqrt(second_new / corr_two) + adam_eps
    )
    return (weight_new, moment_new, second_new)


def adam_kernel(parts_ref, gain_ref, *refs):
    ins, outs = refs[:6], refs[6:]
    total = jnp.sum(parts_ref[...].astype(F32), axis=0)
    grads = ((total[:RANK] * gain_ref[...]).T, total[RANK:])
    for first, grad in zip((0, 3), grads):
        updated = adam_update(*(ref[0] for ref in ins[first : first + 3]), grad)
        for ref, value in zip(outs[first : first + 3], updated):
            ref[0] = value


def adam(parts, gain, state):
    return pl.pallas_call(
        adam_kernel,
        out_shape=tuple(jax.ShapeDtypeStruct(value.shape, F32) for value in state),
        in_specs=[VMEM] * 8,
        out_specs=(VMEM,) * 6,
        compiler_params=params(32),
        cost_estimate=cost(2**22, 5 * 2**20),
    )(parts, gain, *state)


def per_device(
    micro_inputs,
    cotangent,
    norm_gain,
    enter_weight,
    enter_moment,
    enter_second,
    leave_weight,
    leave_moment,
    leave_second,
):
    section = lax.axis_index(SECTION)
    part = lax.axis_index(DP)
    core = lax.axis_index("c")
    index = jnp.stack([section, core, lax.axis_index("xh"), lax.axis_index("y")])
    gain = lax.dynamic_slice_in_dim(norm_gain, part * SLICE, SLICE, axis=1).astype(F32)
    swap = [(0, 1), (1, 0)]
    up = [(i, (i + 1) % 4) for i in range(4)]
    down = [(i, (i + 3) % 4) for i in range(4)]

    def exchange(value, axes):
        return lax.all_to_all(value, axes, split_axis=0, concat_axis=0, tiled=True)

    def spread(value):
        return exchange(jnp.broadcast_to(value[None], (PARTS,) + value.shape), DP)

    with jax.named_scope("weights"):
        near = exchange(own_weights(enter_weight, leave_weight, gain), ("xh", "y"))
        far = lax.ppermute(near, "c", swap)

    with jax.named_scope("gram"):
        both = jnp.concatenate(
            [
                lax.dynamic_slice_in_dim(
                    value.reshape(CHUNK, WIDTH), section * OWN_ROWS, OWN_ROWS, 0
                )
                for value in (micro_inputs, cotangent)
            ]
        )
        packed = exchange(gram_and_rows(index, near, far, both), DP)
        blocks = spread(jnp.sum(packed[:, :PIECE, :].astype(F32), axis=0).astype(BF))
        blocks = blocks.reshape(HALF, RANK, LANES)
        other = lax.ppermute(blocks, "xh", swap)

    with jax.named_scope("project"):
        proj, rows, grads, square = project(index, packed, near, far)

        def ring(value):
            below = lax.ppermute(value, "y", up)
            above = lax.ppermute(value, "y", down)
            return [value, above, lax.ppermute(above, "y", down), below]

        plane = ring(blocks)
        other, _ = lax.optimization_barrier((other, proj))
        gram = plane + ring(other)
        gram = gram + [lax.ppermute(value, "c", swap) for value in gram]
        proj, _, _ = lax.optimization_barrier((exchange(proj, DP), other, plane[2]))
        proj = spread(jnp.sum(proj.astype(F32), axis=0).astype(BF))

    with jax.named_scope("chain"):
        keep, other = chain(index, gram, proj, square, near, far, rows, grads)

    with jax.named_scope("sum"):
        received = lax.ppermute(other, "c", swap)
        parts = exchange((keep.astype(F32) + received.astype(F32)).astype(BF), ("xh", "y"))

    with jax.named_scope("adam"):
        return adam(
            parts,
            gain,
            (enter_weight, enter_moment, enter_second, leave_weight, leave_moment, leave_second),
        )


def solution(mesh):
    split = Mesh(mesh.devices.reshape(2, 4, 2, 2, 8), SECTION + DP)
    rows = P(None, None, DP, None)
    enter = P(SECTION, DP, None)
    leave = P(SECTION, None, DP)
    return jax.shard_map(
        per_device,
        mesh=split,
        in_specs=(rows, rows, P(SECTION, None)) + (enter,) * 3 + (leave,) * 3,
        out_specs=(enter,) * 3 + (leave,) * 3,
        check_vma=False,
    )
```

```python
import jax
import jax.numpy as jnp
from jax import lax
from jax.experimental import pallas as pl
from jax.experimental.pallas import tpu as pltpu
from jax.sharding import Mesh, PartitionSpec as P

eps_norm = 1e-05
rate = 0.001
beta_one = 0.9
beta_two = 0.95
adam_eps = 1e-08
step_count = 10

LAYERS = 16
RANK = 128
WIDTH = 8192
PARTS = 16
SLICE = WIDTH // PARTS
CHUNK = 128
OWN_ROWS = CHUNK // PARTS
HALF = LAYERS // 2
PIECE = HALF * RANK // PARTS
LANES = 2 * RANK
SPANS = SLICE // LANES
TAIL = SPANS * 2 * OWN_ROWS
PACKED = TAIL + 2 * OWN_ROWS
STACKED = (HALF + 1 + LAYERS // 2) * RANK

SECTION = ("xh", "y", "c")
DP = ("xl", "z")

BF = jnp.bfloat16
F32 = jnp.float32


def nn(a, b):
    return lax.dot_general(a, b, (((1,), (0,)), ((), ())), preferred_element_type=F32)


def nt(a, b):
    return lax.dot_general(a, b, (((1,), (1,)), ((), ())), preferred_element_type=F32)


def tn(a, b):
    return lax.dot_general(a, b, (((0,), (0,)), ((), ())), preferred_element_type=F32)


VMEM = pl.BlockSpec(memory_space=pltpu.VMEM)
SMEM = pl.BlockSpec(memory_space=pltpu.SMEM)
ANY = pl.BlockSpec(memory_space=pl.ANY)
HBM = pl.BlockSpec(memory_space=pltpu.HBM)


def params(mebibytes):
    return pltpu.CompilerParams(vmem_limit_bytes=mebibytes * 2**20)


def cost(flops, bytes_accessed):
    return pl.CostEstimate(flops=flops, bytes_accessed=bytes_accessed, transcendentals=0)


def own_kernel(enter_ref, leave_ref, gain_ref, out_ref):
    enter = enter_ref[0].astype(BF).astype(F32).T * gain_ref[...]
    out_ref[:RANK, :] = enter.astype(BF)
    out_ref[RANK:, :] = leave_ref[0].astype(BF)


def own_weights(enter_weight, leave_weight, gain):
    return pl.pallas_call(
        own_kernel,
        out_shape=jax.ShapeDtypeStruct((2 * RANK, SLICE), BF),
        in_specs=[VMEM] * 3,
        out_specs=VMEM,
        compiler_params=params(16),
        cost_estimate=cost(2**18, 3 * 2**20),
    )(enter_weight, leave_weight, gain)


def source_layers(index_ref):
    core, plane, ring = index_ref[1], index_ref[2], index_ref[3]
    return [
        ((1 - plane if step_plane else plane) * 4 + lax.rem(ring + step_ring, 4)) * 2
        + (1 - core if step_core else core)
        for step_core in range(2)
        for step_plane in range(2)
        for step_ring in range(4)
    ]


def load_weights(index_ref, refs, weights, sems):
    copies = [
        pltpu.make_async_copy(ref, weights.at[layer], sems.at[step])
        for step, (layer, ref) in enumerate(zip(source_layers(index_ref), refs))
    ]
    for copy in copies:
        copy.start()
    return copies


def pack_kernel(both_ref, out_ref):
    both = both_ref[...]
    for part in range(PARTS):
        for span in range(SPANS):
            first = 2 * OWN_ROWS * span
            start = SLICE * part + LANES * span
            out_ref[part, first : first + 2 * OWN_ROWS, :] = both[:, start : start + LANES]
    wide = both.astype(F32)[:OWN_ROWS]
    square = jnp.sum(wide * wide, axis=1, keepdims=True)
    high = square.astype(BF).astype(F32)
    tail = jnp.concatenate(
        [
            jnp.broadcast_to(high, (OWN_ROWS, LANES)),
            jnp.broadcast_to(square - high, (OWN_ROWS, LANES)),
        ],
        axis=0,
    ).astype(BF)
    for part in range(PARTS):
        out_ref[part, TAIL:, :] = tail


def pack_rows(both):
    return pl.pallas_call(
        pack_kernel,
        out_shape=jax.ShapeDtypeStruct((PARTS, PACKED, LANES), BF),
        in_specs=[VMEM],
        out_specs=VMEM,
        compiler_params=params(16),
        cost_estimate=cost(2**18, 2**20),
    )(both)


def gram_kernel(index_ref, *refs):
    weight_refs, (out_ref, weights, sems) = refs[:LAYERS], refs[LAYERS:]
    section = index_ref[0]
    for copy in load_weights(index_ref, weight_refs, weights, sems):
        copy.wait()

    def layer_rows(layer, rows):
        return weights[layer, rows, :]

    leave = pl.ds(RANK, RANK)
    for reach in range(HALF):
        other = lax.rem(section + reach, LAYERS)
        low = layer_rows(jnp.minimum(section, other), leave)
        if reach > 0:
            block = nt(low, layer_rows(jnp.maximum(section, other), pl.ds(0, 2 * RANK)))
        else:
            across = lax.rem(section + HALF, LAYERS)
            start = pl.multiple_of((section // HALF) * RANK, RANK)
            far_rows = layer_rows(jnp.maximum(section, across), pl.ds(start, RANK))
            near_rows = layer_rows(jnp.minimum(section, across), leave)
            block = jnp.concatenate([nt(near_rows, far_rows), nt(low, low)], axis=1)
        block = block.astype(BF)
        out_ref[reach] = block


def gram_blocks(index, weights):
    return pl.pallas_call(
        gram_kernel,
        out_shape=jax.ShapeDtypeStruct((HALF, RANK, LANES), BF),
        in_specs=[SMEM] + [HBM] * LAYERS,
        out_specs=VMEM,
        scratch_shapes=[
            pltpu.VMEM((LAYERS, 2 * RANK, SLICE), BF),
            pltpu.SemaphoreType.DMA((LAYERS,)),
        ],
        compiler_params=params(32),
        cost_estimate=cost(2 * LAYERS * RANK * RANK * SLICE, 6 * 2**20),
    )(index, *weights)


def sum_kernel(parts_ref, out_ref):
    total = jnp.sum(parts_ref[...].astype(F32), axis=0).astype(BF)
    for part in range(PARTS):
        out_ref[part] = total


def sum_and_spread(parts):
    return pl.pallas_call(
        sum_kernel,
        out_shape=jax.ShapeDtypeStruct(parts.shape, BF),
        in_specs=[VMEM],
        out_specs=VMEM,
        compiler_params=params(16),
        cost_estimate=cost(parts.size, 4 * parts.size),
    )(parts)


def project_kernel(index_ref, packed_ref, *refs):
    weight_refs = refs[:LAYERS]
    out_ref, rows_ref, grads_ref, square_ref, weights, sems = refs[LAYERS:]
    copies = load_weights(index_ref, weight_refs, weights, sems)
    lanes = []
    for span in range(SPANS):
        first = 2 * OWN_ROWS * span
        lanes.append(packed_ref[:, first : first + 2 * OWN_ROWS, :].astype(F32))
    both = jnp.concatenate(lanes, axis=2)
    rows = both[:, :OWN_ROWS, :].reshape(CHUNK, SLICE).astype(BF)
    grads = both[:, OWN_ROWS:, :].reshape(CHUNK, SLICE).astype(BF)
    rows_ref[...] = rows
    grads_ref[...] = grads
    tail = packed_ref[:, TAIL:, :RANK].astype(F32)
    square_ref[...] = (tail[:, :OWN_ROWS, :] + tail[:, OWN_ROWS:, :]).reshape(CHUNK, RANK)
    for copy in copies:
        copy.wait()
    for layer in range(LAYERS):
        out_ref[layer, :, : 2 * RANK] = nt(rows, weights[layer]).astype(BF)
        out_ref[layer, :, 2 * RANK :] = nt(grads, weights[layer, RANK:, :]).astype(BF)


def project(index, packed, weights):
    return pl.pallas_call(
        project_kernel,
        out_shape=(
            jax.ShapeDtypeStruct((LAYERS, CHUNK, 3 * RANK), BF),
            jax.ShapeDtypeStruct((CHUNK, SLICE), BF),
            jax.ShapeDtypeStruct((CHUNK, SLICE), BF),
            jax.ShapeDtypeStruct((CHUNK, RANK), F32),
        ),
        in_specs=[SMEM, VMEM] + [HBM] * LAYERS,
        out_specs=(VMEM,) * 4,
        scratch_shapes=[
            pltpu.VMEM((LAYERS, 2 * RANK, SLICE), BF),
            pltpu.SemaphoreType.DMA((LAYERS,)),
        ],
        compiler_params=params(32),
        cost_estimate=cost(2 * CHUNK * SLICE * 3 * RANK * LAYERS, 7 * 2**20),
    )(index, packed, *weights)


def stacked(high):
    if high < HALF:
        return (0, high * LANES)
    return ((LAYERS - high) * RANK, (LAYERS - 1 - high) * LANES)


def chain_kernel(
    index_ref,
    gram,
    proj_ref,
    square_ref,
    weights,
    rows_ref,
    grads_ref,
    keep_ref,
    pass_ref,
    shares,
    hidden,
    back,
    pre_saved,
    leave_saved,
    rows_saved,
    inv_saved,
    out_sems,
):
    core = index_ref[1]

    def block(first, end, high):
        top, lane = stacked(high)
        return gram[top + first * RANK : top + end * RANK, lane : lane + LANES]

    def advance(layer, wide):
        rows_saved[layer] = wide.astype(BF)
        if layer == LAYERS - 1:
            return wide
        act = hidden[:, layer * RANK : (layer + 1) * RANK]
        return wide + nn(act, weights[layer, RANK:, :])

    def leaving(half):
        return (
            pltpu.make_async_copy(shares.at[0, half], keep_ref.at[half], out_sems.at[0, half]),
            pltpu.make_async_copy(shares.at[1, half], pass_ref.at[half], out_sems.at[1, half]),
        )

    square = square_ref[...][:, :1]
    wide = rows_ref[...].astype(F32)
    for layer in range(LAYERS):
        total = proj_ref[layer, :, : 2 * RANK].astype(F32)
        if layer > 1:
            before = (layer - 1) * RANK
            total = total + nn(hidden[:, :before], block(0, layer - 1, layer))
        if layer > 0:
            near = slice((layer - 1) * RANK, layer * RANK)
            total = total + nn(hidden[:, near], block(layer - 1, layer, layer))
        inverse = lax.rsqrt(square * (1.0 / WIDTH) + eps_norm)
        pre_act = total[:, :RANK] * inverse
        act = (pre_act * jax.nn.sigmoid(pre_act)).astype(BF)
        own = slice(layer * RANK, (layer + 1) * RANK)
        hidden[:, own] = act
        pre_saved[layer] = pre_act
        inv_saved[layer] = jnp.broadcast_to(inverse, (CHUNK, RANK))
        leave_now = total[:, RANK:]
        leave_next = leave_now + nn(act, block(layer, layer + 1, layer)[:, RANK:])
        leave_saved[layer] = leave_next
        square = jnp.maximum(
            square
            + jnp.sum(act.astype(F32) * (leave_now + leave_next), axis=1, keepdims=True),
            0.0,
        )
        wide = advance(layer, wide)

    drain = jnp.zeros((CHUNK, 1), F32)
    incoming = grads_ref[...].astype(F32)
    for layer in range(LAYERS - 1, -1, -1):
        own = slice(layer * RANK, (layer + 1) * RANK)
        total = proj_ref[layer, :, 2 * RANK :].astype(F32)
        if layer < LAYERS - 2:
            lanes = slice(2 * (layer + 2) * RANK, 2 * LAYERS * RANK)
            later = [block(layer, layer + 1, high) for high in range(layer + 2, LAYERS)]
            total = total + nt(back[:, lanes], jnp.concatenate(later, axis=1))
        if layer < LAYERS - 1:
            near = slice(2 * (layer + 1) * RANK, 2 * (layer + 2) * RANK)
            total = total + nt(back[:, near], block(layer, layer + 1, layer + 1))
        pre_act = pre_saved[layer]
        inverse = inv_saved[layer]
        hidden_grad = total - drain * leave_saved[layer]
        sig_act = jax.nn.sigmoid(pre_act)
        inner = hidden_grad * (sig_act * (1.0 + pre_act * (1.0 - sig_act)))
        inner = inner.astype(BF).astype(F32)
        unit = (inner * inverse).astype(BF)
        act = hidden[:, own]
        back[:, 2 * layer * RANK : (2 * layer + 1) * RANK] = unit
        back[:, (2 * layer + 1) * RANK : (2 * layer + 2) * RANK] = (
            -drain * act.astype(F32)
        ).astype(BF)
        share = (
            jnp.sum(inner * pre_act, axis=1, keepdims=True)
            * (inverse[:, :1] * inverse[:, :1])
            * (1.0 / WIDTH)
        )
        drain = drain + share
        layer_rows = rows_saved[layer]
        side = core if layer % 2 == 0 else 1 - core
        shares[side, layer // 2, :RANK, :] = tn(unit, layer_rows).astype(BF)
        shares[side, layer // 2, RANK:, :] = tn(act, incoming.astype(BF)).astype(BF)
        if layer > 0:
            incoming = (
                incoming
                + nn(unit, weights[layer, :RANK, :])
                - share * layer_rows.astype(F32)
            )
        if layer % 2 == 0:
            for copy in leaving(layer // 2):
                copy.start()
    for half in range(HALF):
        for copy in leaving(half):
            copy.wait()


def place_kernel(index_ref, *refs):
    weight_refs, block_refs = refs[:LAYERS], refs[LAYERS : 2 * LAYERS]
    gram, weights, sem, weight_sems = refs[2 * LAYERS :]
    started = []
    loads = load_weights(index_ref, weight_refs, weights, weight_sems)

    def place(ref, low, high, lane, width):
        early = high < HALF
        top = jnp.where(early, low, low + LAYERS - high)
        rows = pl.ds(pl.multiple_of(top * RANK, RANK), RANK)
        first = jnp.where(early, 2 * high, 2 * (LAYERS - 1 - high)) + lane
        lanes = pl.ds(pl.multiple_of(first * RANK, RANK), width)
        copy = pltpu.make_async_copy(ref, gram.at[rows, lanes], sem.at[len(started)])
        copy.start()
        started.append(copy)

    for layer, block_ref in zip(source_layers(index_ref), block_refs):
        place(block_ref.at[0, :, pl.ds(RANK, RANK)], layer, layer, 1, RANK)
        for reach in range(1, HALF):
            other = lax.rem(layer + reach, LAYERS)
            low, high = jnp.minimum(layer, other), jnp.maximum(layer, other)
            place(block_ref.at[reach], low, high, 0, LANES)
        other = lax.rem(layer + HALF, LAYERS)
        low, high = jnp.minimum(layer, other), jnp.maximum(layer, other)
        place(block_ref.at[0, :, pl.ds(0, RANK)], low, high, layer // HALF, RANK)
    for copy in started + loads:
        copy.wait()


def place_blocks(index, weights, blocks):
    return pl.pallas_call(
        place_kernel,
        out_shape=(
            jax.ShapeDtypeStruct((STACKED, HALF * LANES), BF),
            jax.ShapeDtypeStruct((LAYERS, 2 * RANK, SLICE), BF),
        ),
        in_specs=[SMEM] + [HBM] * (2 * LAYERS),
        out_specs=(VMEM, VMEM),
        scratch_shapes=[
            pltpu.SemaphoreType.DMA((LAYERS * (HALF + 1),)),
            pltpu.SemaphoreType.DMA((LAYERS,)),
        ],
        compiler_params=params(18),
        cost_estimate=cost(2**16, 24 * 2**20),
    )(index, *weights, *blocks)


def chain(index, gram, proj, square, weights, rows, grads):
    side = jax.ShapeDtypeStruct((HALF, 2 * RANK, SLICE), BF)
    return pl.pallas_call(
        chain_kernel,
        out_shape=(side, side),
        in_specs=[SMEM] + [VMEM] * 6,
        out_specs=(ANY, ANY),
        scratch_shapes=[
            pltpu.VMEM((2, HALF, 2 * RANK, SLICE), BF),
            pltpu.VMEM((CHUNK, LAYERS * RANK), BF),
            pltpu.VMEM((CHUNK, 2 * LAYERS * RANK), BF),
            pltpu.VMEM((LAYERS, CHUNK, RANK), F32),
            pltpu.VMEM((LAYERS, CHUNK, RANK), F32),
            pltpu.VMEM((LAYERS, CHUNK, SLICE), BF),
            pltpu.VMEM((LAYERS, CHUNK, RANK), F32),
            pltpu.SemaphoreType.DMA((2, HALF)),
        ],
        compiler_params=params(32),
        cost_estimate=cost(4 * 2**30, 20 * 2**20),
    )(index, gram, proj, square, weights, rows, grads)


def adam_update(weight, moment, second, grad):
    moment_new = beta_one * moment + (1.0 - beta_one) * grad
    second_new = beta_two * second + (1.0 - beta_two) * grad * grad
    corr_one = 1.0 - beta_one**step_count
    corr_two = 1.0 - beta_two**step_count
    weight_new = weight - rate * (moment_new / corr_one) / (
        jnp.sqrt(second_new / corr_two) + adam_eps
    )
    return (weight_new, moment_new, second_new)


def adam_kernel(parts_ref, gain_ref, *refs):
    ins, outs = refs[:6], refs[6:]
    total = jnp.sum(parts_ref[...].astype(F32), axis=0)
    grads = ((total[:RANK] * gain_ref[...]).T, total[RANK:])
    for first, grad in zip((0, 3), grads):
        updated = adam_update(*(ref[0] for ref in ins[first : first + 3]), grad)
        for ref, value in zip(outs[first : first + 3], updated):
            ref[0] = value


def adam(parts, gain, state):
    return pl.pallas_call(
        adam_kernel,
        out_shape=tuple(jax.ShapeDtypeStruct(value.shape, F32) for value in state),
        in_specs=[VMEM] * 8,
        out_specs=(VMEM,) * 6,
        compiler_params=params(32),
        cost_estimate=cost(2**22, 5 * 2**20),
    )(parts, gain, *state)


def per_device(
    micro_inputs,
    cotangent,
    norm_gain,
    enter_weight,
    enter_moment,
    enter_second,
    leave_weight,
    leave_moment,
    leave_second,
):
    section = lax.axis_index(SECTION)
    part = lax.axis_index(DP)
    core = lax.axis_index("c")
    index = jnp.stack([section, core, lax.axis_index("xh"), lax.axis_index("y")])
    gain = lax.dynamic_slice_in_dim(norm_gain, part * SLICE, SLICE, axis=1).astype(F32)
    swap = [(0, 1), (1, 0)]
    up = [(i, (i + 1) % 4) for i in range(4)]
    down = [(i, (i + 3) % 4) for i in range(4)]

    def exchange(value, axes):
        return lax.all_to_all(value, axes, split_axis=0, concat_axis=0, tiled=True)

    def ring(value):
        below = lax.ppermute(value, "y", up)
        above = lax.ppermute(value, "y", down)
        return [value, above, lax.ppermute(above, "y", down), below]

    def cores(values):
        return values + [lax.ppermute(value, "c", swap) for value in values]

    with jax.named_scope("weights"):
        mine = own_weights(enter_weight, leave_weight, gain)
        weights = cores(ring(mine) + ring(lax.ppermute(mine, "xh", swap)))

    with jax.named_scope("rows"):
        both = jnp.concatenate(
            [
                lax.dynamic_slice_in_dim(
                    value.reshape(CHUNK, WIDTH), section * OWN_ROWS, OWN_ROWS, 0
                )
                for value in (micro_inputs, cotangent)
            ]
        )
        packed = exchange(pack_rows(both), DP)

    with jax.named_scope("gram"):
        after, _ = lax.optimization_barrier((index, packed))
        blocks = gram_blocks(after, weights).reshape(PARTS, PIECE, LANES)
        blocks = exchange(sum_and_spread(exchange(blocks, DP)), DP)
        blocks = blocks.reshape(HALF, RANK, LANES)
        other = lax.ppermute(blocks, "xh", swap)

    with jax.named_scope("project"):
        proj, rows, grads, square = project(index, packed, weights)
        near = ring(blocks)
        other, _ = lax.optimization_barrier((other, proj))
        gram = cores(near + ring(other))
        proj, _, _ = lax.optimization_barrier((exchange(proj, DP), other, near[2]))
        proj = exchange(sum_and_spread(proj), DP)
        after, _ = lax.optimization_barrier((index, proj))
        gram, weights = place_blocks(after, weights, gram)

    with jax.named_scope("chain"):
        keep, other = chain(index, gram, proj, square, weights, rows, grads)

    with jax.named_scope("sum"):
        received = lax.ppermute(other, "c", swap)
        parts = exchange((keep.astype(F32) + received.astype(F32)).astype(BF), ("xh", "y"))

    with jax.named_scope("adam"):
        return adam(
            parts,
            gain,
            (enter_weight, enter_moment, enter_second, leave_weight, leave_moment, leave_second),
        )


def solution(mesh):
    split = Mesh(mesh.devices.reshape(2, 4, 2, 2, 8), SECTION + DP)
    rows = P(None, None, DP, None)
    enter = P(SECTION, DP, None)
    leave = P(SECTION, None, DP)
    return jax.shard_map(
        per_device,
        mesh=split,
        in_specs=(rows, rows, P(SECTION, None)) + (enter,) * 3 + (leave,) * 3,
        out_specs=(enter,) * 3 + (leave,) * 3,
        check_vma=False,
    )
```

```python
import jax
import jax.numpy as jnp
from jax import lax
from jax.experimental import pallas as pl
from jax.experimental.pallas import tpu as pltpu
from jax.sharding import Mesh, PartitionSpec as P

eps_norm = 1e-05
rate = 0.001
beta_one = 0.9
beta_two = 0.95
adam_eps = 1e-08
step_count = 10

LAYERS = 16
RANK = 128
WIDTH = 8192
PARTS = 16
SLICE = WIDTH // PARTS
CHUNK = 128
OWN_ROWS = CHUNK // PARTS
HALF = LAYERS // 2
PIECE = HALF * RANK // PARTS
LANES = 2 * RANK
SPANS = SLICE // LANES
TAIL = PIECE + SPANS * 2 * OWN_ROWS
PACKED = TAIL + 2 * OWN_ROWS
STACKED = (HALF + 1 + LAYERS // 2) * RANK

SECTION = ("xh", "y", "c")
DP = ("xl", "z")

BF = jnp.bfloat16
F32 = jnp.float32


def nn(a, b):
    return lax.dot_general(a, b, (((1,), (0,)), ((), ())), preferred_element_type=F32)


def nt(a, b):
    return lax.dot_general(a, b, (((1,), (1,)), ((), ())), preferred_element_type=F32)


def tn(a, b):
    return lax.dot_general(a, b, (((0,), (0,)), ((), ())), preferred_element_type=F32)


VMEM = pl.BlockSpec(memory_space=pltpu.VMEM)
SMEM = pl.BlockSpec(memory_space=pltpu.SMEM)
ANY = pl.BlockSpec(memory_space=pl.ANY)
HBM = pl.BlockSpec(memory_space=pltpu.HBM)


def params(mebibytes):
    return pltpu.CompilerParams(vmem_limit_bytes=mebibytes * 2**20)


def cost(flops, bytes_accessed):
    return pl.CostEstimate(flops=flops, bytes_accessed=bytes_accessed, transcendentals=0)


def own_kernel(enter_ref, leave_ref, gain_ref, out_ref):
    enter = enter_ref[0].astype(BF).astype(F32).T * gain_ref[...]
    enter = enter.astype(BF)
    leave = leave_ref[0].astype(BF)
    for copy in range(HALF):
        out_ref[copy, :RANK, :] = enter
        out_ref[copy, RANK:, :] = leave


def own_weights(enter_weight, leave_weight, gain):
    return pl.pallas_call(
        own_kernel,
        out_shape=jax.ShapeDtypeStruct((HALF, 2 * RANK, SLICE), BF),
        in_specs=[VMEM] * 3,
        out_specs=VMEM,
        compiler_params=params(16),
        cost_estimate=cost(2**18, 3 * 2**20),
    )(enter_weight, leave_weight, gain)


def load_weights(core, near_ref, far_ref, weights, sems):
    copies = [
        pltpu.make_async_copy(near_ref, weights.at[core], sems.at[0]),
        pltpu.make_async_copy(far_ref, weights.at[1 - core], sems.at[1]),
    ]
    for copy in copies:
        copy.start()
    return copies


def gram_kernel(index_ref, near_ref, far_ref, both_ref, out_ref, weights, sems):
    section = index_ref[0]
    copies = load_weights(index_ref[1], near_ref, far_ref, weights, sems)
    both = both_ref[...]
    for part in range(PARTS):
        for span in range(SPANS):
            first = PIECE + 2 * OWN_ROWS * span
            start = SLICE * part + LANES * span
            out_ref[part, first : first + 2 * OWN_ROWS, :] = both[:, start : start + LANES]
    wide = both.astype(F32)[:OWN_ROWS]
    square = jnp.sum(wide * wide, axis=1, keepdims=True)
    high = square.astype(BF).astype(F32)
    tail = jnp.concatenate(
        [
            jnp.broadcast_to(high, (OWN_ROWS, LANES)),
            jnp.broadcast_to(square - high, (OWN_ROWS, LANES)),
        ],
        axis=0,
    ).astype(BF)
    for part in range(PARTS):
        out_ref[part, TAIL:, :] = tail
    for copy in copies:
        copy.wait()

    def layer_rows(layer, rows):
        return weights[lax.rem(layer, 2), layer // 2, rows, :]

    leave = pl.ds(RANK, RANK)
    for reach in range(HALF):
        other = lax.rem(section + reach, LAYERS)
        low = layer_rows(jnp.minimum(section, other), leave)
        if reach > 0:
            block = nt(low, layer_rows(jnp.maximum(section, other), pl.ds(0, 2 * RANK)))
        else:
            across = lax.rem(section + HALF, LAYERS)
            start = pl.multiple_of((section // HALF) * RANK, RANK)
            far_rows = layer_rows(jnp.maximum(section, across), pl.ds(start, RANK))
            near_rows = layer_rows(jnp.minimum(section, across), leave)
            block = jnp.concatenate([nt(near_rows, far_rows), nt(low, low)], axis=1)
        block = block.astype(BF)
        out_ref[2 * reach, :PIECE, :] = block[:PIECE]
        out_ref[2 * reach + 1, :PIECE, :] = block[PIECE:]


def gram_and_rows(index, near, far, both):
    return pl.pallas_call(
        gram_kernel,
        out_shape=jax.ShapeDtypeStruct((PARTS, PACKED, LANES), BF),
        in_specs=[SMEM, ANY, ANY, VMEM],
        out_specs=VMEM,
        scratch_shapes=[
            pltpu.VMEM((2, HALF, 2 * RANK, SLICE), BF),
            pltpu.SemaphoreType.DMA((2,)),
        ],
        compiler_params=params(32),
        cost_estimate=cost(2 * LAYERS * RANK * RANK * SLICE, 6 * 2**20),
    )(index, near, far, both)


def sum_kernel(parts_ref, out_ref):
    step = 2 * OWN_ROWS

    def body(index, carry):
        rows = pl.ds(pl.multiple_of(index * step, step), step)
        total = jnp.sum(parts_ref[:, rows, :].astype(F32), axis=0).astype(BF)
        for part in range(PARTS):
            out_ref[part, rows, :] = total
        return carry

    lax.fori_loop(0, parts_ref.shape[1] // step, body, 0)


def sum_and_spread(parts):
    return pl.pallas_call(
        sum_kernel,
        out_shape=jax.ShapeDtypeStruct(parts.shape, BF),
        in_specs=[VMEM],
        out_specs=VMEM,
        compiler_params=params(16),
        cost_estimate=cost(parts.size, 4 * parts.size),
    )(parts)


def project_kernel(
    index_ref, packed_ref, near_ref, far_ref, out_ref, rows_ref, grads_ref, square_ref, weights, sems
):
    copies = load_weights(index_ref[1], near_ref, far_ref, weights, sems)
    lanes = []
    for span in range(SPANS):
        first = PIECE + 2 * OWN_ROWS * span
        lanes.append(packed_ref[:, first : first + 2 * OWN_ROWS, :].astype(F32))
    both = jnp.concatenate(lanes, axis=2)
    rows = both[:, :OWN_ROWS, :].reshape(CHUNK, SLICE).astype(BF)
    grads = both[:, OWN_ROWS:, :].reshape(CHUNK, SLICE).astype(BF)
    rows_ref[...] = rows
    grads_ref[...] = grads
    tail = packed_ref[:, TAIL:, :RANK].astype(F32)
    square_ref[...] = (tail[:, :OWN_ROWS, :] + tail[:, OWN_ROWS:, :]).reshape(CHUNK, RANK)
    for copy in copies:
        copy.wait()
    for layer in range(LAYERS):
        place = (layer % 2, layer // 2)
        out_ref[layer, :, : 2 * RANK] = nt(rows, weights[place]).astype(BF)
        out_ref[layer, :, 2 * RANK :] = nt(grads, weights[place][RANK:, :]).astype(BF)


def project(index, packed, near, far):
    return pl.pallas_call(
        project_kernel,
        out_shape=(
            jax.ShapeDtypeStruct((LAYERS, CHUNK, 3 * RANK), BF),
            jax.ShapeDtypeStruct((CHUNK, SLICE), BF),
            jax.ShapeDtypeStruct((CHUNK, SLICE), BF),
            jax.ShapeDtypeStruct((CHUNK, RANK), F32),
        ),
        in_specs=[SMEM, VMEM, ANY, ANY],
        out_specs=(VMEM,) * 4,
        scratch_shapes=[
            pltpu.VMEM((2, HALF, 2 * RANK, SLICE), BF),
            pltpu.SemaphoreType.DMA((2,)),
        ],
        compiler_params=params(32),
        cost_estimate=cost(2 * CHUNK * SLICE * 3 * RANK * LAYERS, 7 * 2**20),
    )(index, packed, near, far)


def stacked(high):
    if high < HALF:
        return (0, high * LANES)
    return ((LAYERS - high) * RANK, (LAYERS - 1 - high) * LANES)


def chain_kernel(
    index_ref,
    gram,
    proj_ref,
    square_ref,
    weights,
    rows_ref,
    grads_ref,
    keep_ref,
    pass_ref,
    shares,
    hidden,
    back,
    pre_saved,
    leave_saved,
    rows_saved,
    inv_saved,
    out_sems,
):
    core = index_ref[1]

    def block(first, end, high):
        top, lane = stacked(high)
        return gram[top + first * RANK : top + end * RANK, lane : lane + LANES]

    def advance(layer, wide):
        rows_saved[layer] = wide.astype(BF)
        if layer == LAYERS - 1:
            return wide
        act = hidden[:, layer * RANK : (layer + 1) * RANK]
        return wide + nn(act, weights[layer % 2, layer // 2, RANK:, :])

    def leaving(half):
        return (
            pltpu.make_async_copy(shares.at[0, half], keep_ref.at[half], out_sems.at[0, half]),
            pltpu.make_async_copy(shares.at[1, half], pass_ref.at[half], out_sems.at[1, half]),
        )

    square = square_ref[...][:, :1]
    wide = rows_ref[...].astype(F32)
    for layer in range(LAYERS):
        total = proj_ref[layer, :, : 2 * RANK].astype(F32)
        if layer > 1:
            before = (layer - 1) * RANK
            total = total + nn(hidden[:, :before], block(0, layer - 1, layer))
        if layer > 0:
            near = slice((layer - 1) * RANK, layer * RANK)
            total = total + nn(hidden[:, near], block(layer - 1, layer, layer))
        inverse = lax.rsqrt(square * (1.0 / WIDTH) + eps_norm)
        pre_act = total[:, :RANK] * inverse
        act = (pre_act * jax.nn.sigmoid(pre_act)).astype(BF)
        own = slice(layer * RANK, (layer + 1) * RANK)
        hidden[:, own] = act
        pre_saved[layer] = pre_act
        inv_saved[layer] = jnp.broadcast_to(inverse, (CHUNK, RANK))
        leave_now = total[:, RANK:]
        leave_next = leave_now + nn(act, block(layer, layer + 1, layer)[:, RANK:])
        leave_saved[layer] = leave_next
        square = jnp.maximum(
            square
            + jnp.sum(act.astype(F32) * (leave_now + leave_next), axis=1, keepdims=True),
            0.0,
        )
        wide = advance(layer, wide)

    drain = jnp.zeros((CHUNK, 1), F32)
    incoming = grads_ref[...].astype(F32)
    for layer in range(LAYERS - 1, -1, -1):
        own = slice(layer * RANK, (layer + 1) * RANK)
        total = proj_ref[layer, :, 2 * RANK :].astype(F32)
        if layer < LAYERS - 2:
            lanes = slice(2 * (layer + 2) * RANK, 2 * LAYERS * RANK)
            later = [block(layer, layer + 1, high) for high in range(layer + 2, LAYERS)]
            total = total + nt(back[:, lanes], jnp.concatenate(later, axis=1))
        if layer < LAYERS - 1:
            near = slice(2 * (layer + 1) * RANK, 2 * (layer + 2) * RANK)
            total = total + nt(back[:, near], block(layer, layer + 1, layer + 1))
        pre_act = pre_saved[layer]
        inverse = inv_saved[layer]
        hidden_grad = total - drain * leave_saved[layer]
        sig_act = jax.nn.sigmoid(pre_act)
        inner = hidden_grad * (sig_act * (1.0 + pre_act * (1.0 - sig_act)))
        inner = inner.astype(BF).astype(F32)
        unit = (inner * inverse).astype(BF)
        act = hidden[:, own]
        back[:, 2 * layer * RANK : (2 * layer + 1) * RANK] = unit
        back[:, (2 * layer + 1) * RANK : (2 * layer + 2) * RANK] = (
            -drain * act.astype(F32)
        ).astype(BF)
        share = (
            jnp.sum(inner * pre_act, axis=1, keepdims=True)
            * (inverse[:, :1] * inverse[:, :1])
            * (1.0 / WIDTH)
        )
        drain = drain + share
        layer_rows = rows_saved[layer]
        side = core if layer % 2 == 0 else 1 - core
        shares[side, layer // 2, :RANK, :] = tn(unit, layer_rows).astype(BF)
        shares[side, layer // 2, RANK:, :] = tn(act, incoming.astype(BF)).astype(BF)
        if layer > 0:
            incoming = (
                incoming
                + nn(unit, weights[layer % 2, layer // 2, :RANK, :])
                - share * layer_rows.astype(F32)
            )
        if layer % 2 == 0:
            for copy in leaving(layer // 2):
                copy.start()
    for half in range(HALF):
        for copy in leaving(half):
            copy.wait()


def place_kernel(index_ref, near_ref, far_ref, *refs):
    block_refs, (gram, weights, sem, weight_sems) = refs[:LAYERS], refs[LAYERS:]
    core, plane, ring = index_ref[1], index_ref[2], index_ref[3]
    loads = load_weights(core, near_ref, far_ref, weights, weight_sems)
    layers = [
        ((1 - plane if step_plane else plane) * 4 + lax.rem(ring + step_ring, 4)) * 2
        + (1 - core if step_core else core)
        for step_core in range(2)
        for step_plane in range(2)
        for step_ring in range(4)
    ]

    def place(ref, low, high, lane, width, slot):
        early = high < HALF
        top = jnp.where(early, low, low + LAYERS - high)
        rows = pl.ds(pl.multiple_of(top * RANK, RANK), RANK)
        first = jnp.where(early, 2 * high, 2 * (LAYERS - 1 - high)) + lane
        lanes = pl.ds(pl.multiple_of(first * RANK, RANK), width)
        return pltpu.make_async_copy(ref, gram.at[rows, lanes], sem.at[slot])

    def copies(step, layer, block_ref, reach):
        other = lax.rem(layer + reach, LAYERS)
        low, high = jnp.minimum(layer, other), jnp.maximum(layer, other)
        return place(block_ref.at[reach], low, high, 0, LANES, step * (HALF + 1) + reach)

    def halves(step, layer, block_ref):
        other = lax.rem(layer + HALF, LAYERS)
        low, high = jnp.minimum(layer, other), jnp.maximum(layer, other)
        first, slot = block_ref.at[0], step * (HALF + 1)
        return (
            place(first.at[:, pl.ds(RANK, RANK)], layer, layer, 1, RANK, slot),
            place(first.at[:, pl.ds(0, RANK)], low, high, layer // HALF, RANK, slot + HALF),
        )

    sources = list(zip(range(LAYERS), layers, block_refs))
    for source in sources:
        for copy in halves(*source):
            copy.start()

        @pl.loop(1, HALF)
        def _(reach):
            copies(*source, reach).start()

    for source in sources:
        for copy in halves(*source):
            copy.wait()

        @pl.loop(1, HALF)
        def _(reach):
            copies(*source, reach).wait()

    for copy in loads:
        copy.wait()


def place_blocks(index, near, far, blocks):
    return pl.pallas_call(
        place_kernel,
        out_shape=(
            jax.ShapeDtypeStruct((STACKED, HALF * LANES), BF),
            jax.ShapeDtypeStruct((2, HALF, 2 * RANK, SLICE), BF),
        ),
        in_specs=[SMEM] + [HBM] * (LAYERS + 2),
        out_specs=(VMEM, VMEM),
        scratch_shapes=[
            pltpu.SemaphoreType.DMA((LAYERS * (HALF + 1),)),
            pltpu.SemaphoreType.DMA((2,)),
        ],
        compiler_params=params(18),
        cost_estimate=cost(2**16, 24 * 2**20),
    )(index, near, far, *blocks)


def chain(index, gram, proj, square, weights, rows, grads):
    side = jax.ShapeDtypeStruct((HALF, 2 * RANK, SLICE), BF)
    return pl.pallas_call(
        chain_kernel,
        out_shape=(side, side),
        in_specs=[SMEM] + [VMEM] * 6,
        out_specs=(ANY, ANY),
        scratch_shapes=[
            pltpu.VMEM((2, HALF, 2 * RANK, SLICE), BF),
            pltpu.VMEM((CHUNK, LAYERS * RANK), BF),
            pltpu.VMEM((CHUNK, 2 * LAYERS * RANK), BF),
            pltpu.VMEM((LAYERS, CHUNK, RANK), F32),
            pltpu.VMEM((LAYERS, CHUNK, RANK), F32),
            pltpu.VMEM((LAYERS, CHUNK, SLICE), BF),
            pltpu.VMEM((LAYERS, CHUNK, RANK), F32),
            pltpu.SemaphoreType.DMA((2, HALF)),
        ],
        compiler_params=params(32),
        cost_estimate=cost(4 * 2**30, 20 * 2**20),
    )(index, gram, proj, square, weights, rows, grads)


def adam_update(weight, moment, second, grad):
    moment_new = beta_one * moment + (1.0 - beta_one) * grad
    second_new = beta_two * second + (1.0 - beta_two) * grad * grad
    corr_one = 1.0 - beta_one**step_count
    corr_two = 1.0 - beta_two**step_count
    weight_new = weight - rate * (moment_new / corr_one) / (
        jnp.sqrt(second_new / corr_two) + adam_eps
    )
    return (weight_new, moment_new, second_new)


def adam_kernel(parts_ref, gain_ref, *refs):
    ins, outs = refs[:6], refs[6:]
    total = jnp.sum(parts_ref[...].astype(F32), axis=0)
    grads = ((total[:RANK] * gain_ref[...]).T, total[RANK:])
    for first, grad in zip((0, 3), grads):
        updated = adam_update(*(ref[0] for ref in ins[first : first + 3]), grad)
        for ref, value in zip(outs[first : first + 3], updated):
            ref[0] = value


def adam(parts, gain, state):
    return pl.pallas_call(
        adam_kernel,
        out_shape=tuple(jax.ShapeDtypeStruct(value.shape, F32) for value in state),
        in_specs=[VMEM] * 8,
        out_specs=(VMEM,) * 6,
        compiler_params=params(32),
        cost_estimate=cost(2**22, 5 * 2**20),
    )(parts, gain, *state)


def per_device(
    micro_inputs,
    cotangent,
    norm_gain,
    enter_weight,
    enter_moment,
    enter_second,
    leave_weight,
    leave_moment,
    leave_second,
):
    section = lax.axis_index(SECTION)
    part = lax.axis_index(DP)
    core = lax.axis_index("c")
    index = jnp.stack([section, core, lax.axis_index("xh"), lax.axis_index("y")])
    gain = lax.dynamic_slice_in_dim(norm_gain, part * SLICE, SLICE, axis=1).astype(F32)
    swap = [(0, 1), (1, 0)]
    up = [(i, (i + 1) % 4) for i in range(4)]
    down = [(i, (i + 3) % 4) for i in range(4)]

    def exchange(value, axes):
        return lax.all_to_all(value, axes, split_axis=0, concat_axis=0, tiled=True)

    def spread(value):
        return exchange(jnp.broadcast_to(value[None], (PARTS,) + value.shape), DP)

    with jax.named_scope("weights"):
        near = exchange(own_weights(enter_weight, leave_weight, gain), ("xh", "y"))
        far = lax.ppermute(near, "c", swap)

    with jax.named_scope("gram"):
        both = jnp.concatenate(
            [
                lax.dynamic_slice_in_dim(
                    value.reshape(CHUNK, WIDTH), section * OWN_ROWS, OWN_ROWS, 0
                )
                for value in (micro_inputs, cotangent)
            ]
        )
        packed = exchange(gram_and_rows(index, near, far, both), DP)
        blocks = spread(jnp.sum(packed[:, :PIECE, :].astype(F32), axis=0).astype(BF))
        blocks = blocks.reshape(HALF, RANK, LANES)
        other = lax.ppermute(blocks, "xh", swap)

    with jax.named_scope("project"):
        proj, rows, grads, square = project(index, packed, near, far)

        def ring(value):
            below = lax.ppermute(value, "y", up)
            above = lax.ppermute(value, "y", down)
            return [value, above, lax.ppermute(above, "y", down), below]

        plane = ring(blocks)
        other, _ = lax.optimization_barrier((other, proj))
        gram = plane + ring(other)
        gram = gram + [lax.ppermute(value, "c", swap) for value in gram]
        proj, _, _ = lax.optimization_barrier((exchange(proj, DP), other, plane[2]))
        proj = exchange(sum_and_spread(proj), DP)
        after, _ = lax.optimization_barrier((index, proj))
        gram, weights = place_blocks(after, near, far, gram)

    with jax.named_scope("chain"):
        keep, other = chain(index, gram, proj, square, weights, rows, grads)

    with jax.named_scope("sum"):
        received = lax.ppermute(other, "c", swap)
        parts = exchange((keep.astype(F32) + received.astype(F32)).astype(BF), ("xh", "y"))

    with jax.named_scope("adam"):
        return adam(
            parts,
            gain,
            (enter_weight, enter_moment, enter_second, leave_weight, leave_moment, leave_second),
        )


def solution(mesh):
    split = Mesh(mesh.devices.reshape(2, 4, 2, 2, 8), SECTION + DP)
    rows = P(None, None, DP, None)
    enter = P(SECTION, DP, None)
    leave = P(SECTION, None, DP)
    return jax.shard_map(
        per_device,
        mesh=split,
        in_specs=(rows, rows, P(SECTION, None)) + (enter,) * 3 + (leave,) * 3,
        out_specs=(enter,) * 3 + (leave,) * 3,
        check_vma=False,
    )
```

```python
import jax
import jax.numpy as jnp
from jax import lax
from jax.experimental import pallas as pl
from jax.experimental.pallas import tpu as pltpu
from jax.sharding import Mesh, PartitionSpec as P

eps_norm = 1e-05
rate = 0.001
beta_one = 0.9
beta_two = 0.95
adam_eps = 1e-08
step_count = 10

LAYERS = 16
RANK = 128
WIDTH = 8192
PARTS = 16
SLICE = WIDTH // PARTS
CHUNK = 128
OWN_ROWS = CHUNK // PARTS
HALF = LAYERS // 2
PIECE = HALF * RANK // PARTS
LANES = 2 * RANK
SPANS = SLICE // LANES
TAIL = PIECE + SPANS * 2 * OWN_ROWS
PACKED = TAIL + 2 * OWN_ROWS

SECTION = ("xh", "y", "c")
DP = ("xl", "z")

BF = jnp.bfloat16
F32 = jnp.float32


def nn(a, b):
    return lax.dot_general(a, b, (((1,), (0,)), ((), ())), preferred_element_type=F32)


def nt(a, b):
    return lax.dot_general(a, b, (((1,), (1,)), ((), ())), preferred_element_type=F32)


def tn(a, b):
    return lax.dot_general(a, b, (((0,), (0,)), ((), ())), preferred_element_type=F32)


VMEM = pl.BlockSpec(memory_space=pltpu.VMEM)
SMEM = pl.BlockSpec(memory_space=pltpu.SMEM)
ANY = pl.BlockSpec(memory_space=pl.ANY)


def params(mebibytes):
    return pltpu.CompilerParams(vmem_limit_bytes=mebibytes * 2**20)


def cost(flops, bytes_accessed):
    return pl.CostEstimate(flops=flops, bytes_accessed=bytes_accessed, transcendentals=0)


def own_kernel(enter_ref, leave_ref, gain_ref, out_ref):
    enter = enter_ref[0].astype(BF).astype(F32).T * gain_ref[...]
    enter = enter.astype(BF)
    leave = leave_ref[0].astype(BF)
    for copy in range(HALF):
        out_ref[copy, :RANK, :] = enter
        out_ref[copy, RANK:, :] = leave


def own_weights(enter_weight, leave_weight, gain):
    return pl.pallas_call(
        own_kernel,
        out_shape=jax.ShapeDtypeStruct((HALF, 2 * RANK, SLICE), BF),
        in_specs=[VMEM] * 3,
        out_specs=VMEM,
        compiler_params=params(16),
        cost_estimate=cost(2**18, 3 * 2**20),
    )(enter_weight, leave_weight, gain)


def load_weights(core, near_ref, far_ref, weights, sems):
    copies = [
        pltpu.make_async_copy(near_ref, weights.at[core], sems.at[0]),
        pltpu.make_async_copy(far_ref, weights.at[1 - core], sems.at[1]),
    ]
    for copy in copies:
        copy.start()
    return copies


def gram_kernel(index_ref, near_ref, far_ref, both_ref, out_ref, weights, sems):
    section = index_ref[0]
    copies = load_weights(index_ref[1], near_ref, far_ref, weights, sems)
    both = both_ref[...]
    for part in range(PARTS):
        for span in range(SPANS):
            first = PIECE + 2 * OWN_ROWS * span
            start = SLICE * part + LANES * span
            out_ref[part, first : first + 2 * OWN_ROWS, :] = both[:, start : start + LANES]
    wide = both.astype(F32)[:OWN_ROWS]
    square = jnp.sum(wide * wide, axis=1, keepdims=True)
    high = square.astype(BF).astype(F32)
    tail = jnp.concatenate(
        [
            jnp.broadcast_to(high, (OWN_ROWS, LANES)),
            jnp.broadcast_to(square - high, (OWN_ROWS, LANES)),
        ],
        axis=0,
    ).astype(BF)
    for part in range(PARTS):
        out_ref[part, TAIL:, :] = tail
    for copy in copies:
        copy.wait()

    def layer_rows(layer, rows):
        return weights[lax.rem(layer, 2), layer // 2, rows, :]

    leave = pl.ds(RANK, RANK)
    for reach in range(HALF):
        other = lax.rem(section + reach, LAYERS)
        low = layer_rows(jnp.minimum(section, other), leave)
        if reach > 0:
            block = nt(low, layer_rows(jnp.maximum(section, other), pl.ds(0, 2 * RANK)))
        else:
            across = lax.rem(section + HALF, LAYERS)
            start = pl.multiple_of((section // HALF) * RANK, RANK)
            far_rows = layer_rows(jnp.maximum(section, across), pl.ds(start, RANK))
            near_rows = layer_rows(jnp.minimum(section, across), leave)
            block = jnp.concatenate([nt(near_rows, far_rows), nt(low, low)], axis=1)
        block = block.astype(BF)
        out_ref[2 * reach, :PIECE, :] = block[:PIECE]
        out_ref[2 * reach + 1, :PIECE, :] = block[PIECE:]


def gram_and_rows(index, near, far, both):
    return pl.pallas_call(
        gram_kernel,
        out_shape=jax.ShapeDtypeStruct((PARTS, PACKED, LANES), BF),
        in_specs=[SMEM, ANY, ANY, VMEM],
        out_specs=VMEM,
        scratch_shapes=[
            pltpu.VMEM((2, HALF, 2 * RANK, SLICE), BF),
            pltpu.SemaphoreType.DMA((2,)),
        ],
        compiler_params=params(32),
        cost_estimate=cost(2 * LAYERS * RANK * RANK * SLICE, 6 * 2**20),
    )(index, near, far, both)


def project_kernel(
    index_ref, packed_ref, near_ref, far_ref, out_ref, rows_ref, grads_ref, square_ref, weights, sems
):
    copies = load_weights(index_ref[1], near_ref, far_ref, weights, sems)
    lanes = []
    for span in range(SPANS):
        first = PIECE + 2 * OWN_ROWS * span
        lanes.append(packed_ref[:, first : first + 2 * OWN_ROWS, :].astype(F32))
    both = jnp.concatenate(lanes, axis=2)
    rows = both[:, :OWN_ROWS, :].reshape(CHUNK, SLICE).astype(BF)
    grads = both[:, OWN_ROWS:, :].reshape(CHUNK, SLICE).astype(BF)
    rows_ref[...] = rows
    grads_ref[...] = grads
    tail = packed_ref[:, TAIL:, :RANK].astype(F32)
    square_ref[...] = (tail[:, :OWN_ROWS, :] + tail[:, OWN_ROWS:, :]).reshape(CHUNK, RANK)
    for copy in copies:
        copy.wait()
    for layer in range(LAYERS):
        place = (layer % 2, layer // 2)
        out_ref[layer, :, : 2 * RANK] = nt(rows, weights[place]).astype(BF)
        out_ref[layer, :, 2 * RANK :] = nt(grads, weights[place][RANK:, :]).astype(BF)


def project(index, packed, near, far):
    return pl.pallas_call(
        project_kernel,
        out_shape=(
            jax.ShapeDtypeStruct((LAYERS, CHUNK, 3 * RANK), BF),
            jax.ShapeDtypeStruct((CHUNK, SLICE), BF),
            jax.ShapeDtypeStruct((CHUNK, SLICE), BF),
            jax.ShapeDtypeStruct((CHUNK, RANK), F32),
        ),
        in_specs=[SMEM, VMEM, ANY, ANY],
        out_specs=(VMEM,) * 4,
        scratch_shapes=[
            pltpu.VMEM((2, HALF, 2 * RANK, SLICE), BF),
            pltpu.SemaphoreType.DMA((2,)),
        ],
        compiler_params=params(32),
        cost_estimate=cost(2 * CHUNK * SLICE * 3 * RANK * LAYERS, 7 * 2**20),
    )(index, packed, near, far)


def chain_kernel(
    index_ref,
    *refs,
):
    block_refs = refs[:LAYERS]
    (
        proj_ref,
        square_ref,
        near_ref,
        far_ref,
        rows_ref,
        grads_ref,
        keep_ref,
        pass_ref,
        gram,
        weights,
        shares,
        hidden,
        back,
        pre_saved,
        leave_saved,
        rows_saved,
        inv_saved,
        gram_sems,
        sems,
        out_sems,
    ) = refs[LAYERS:]
    core = index_ref[1]
    copies = load_weights(core, near_ref, far_ref, weights, sems)

    plane, ring = index_ref[2], index_ref[3]

    def place(ref, low, high, lane, width):
        rows = pl.ds(pl.multiple_of(low * RANK, RANK), RANK)
        first = pl.multiple_of((2 * high + lane) * RANK, RANK)
        pltpu.make_async_copy(
            ref, gram.at[rows, pl.ds(first, width)], gram_sems.at[high]
        ).start()

    def fetch(block_ref, step_plane, step_ring, step_core):
        across_plane = plane if step_plane == 0 else 1 - plane
        across_core = core if step_core == 0 else 1 - core
        layer = (across_plane * 4 + lax.rem(ring + step_ring, 4)) * 2 + across_core
        place(block_ref.at[0, :, pl.ds(RANK, RANK)], layer, layer, 1, RANK)
        for reach in range(1, HALF):
            other = lax.rem(layer + reach, LAYERS)
            low, high = jnp.minimum(layer, other), jnp.maximum(layer, other)
            place(block_ref.at[reach], low, high, 0, 2 * RANK)
        other = lax.rem(layer + HALF, LAYERS)
        low, high = jnp.minimum(layer, other), jnp.maximum(layer, other)
        place(block_ref.at[0, :, pl.ds(0, RANK)], low, high, layer // HALF, RANK)

    steps = [(core, plane, ring) for core in (0, 1) for plane in (0, 1) for ring in range(4)]
    for (step_core, step_plane, step_ring), block_ref in zip(steps, block_refs):
        fetch(block_ref, step_plane, step_ring, step_core)

    def arrived(layer):
        view = gram.at[pl.ds(0, (2 * layer + 1) * (RANK // 2)), pl.ds(0, 2 * RANK)]
        pltpu.make_async_copy(view, view, gram_sems.at[layer]).wait()

    def leaving(half):
        return (
            pltpu.make_async_copy(shares.at[0, half], keep_ref.at[half], out_sems.at[0, half]),
            pltpu.make_async_copy(shares.at[1, half], pass_ref.at[half], out_sems.at[1, half]),
        )

    square = square_ref[...][:, :1]
    wide = rows_ref[...].astype(F32)
    for layer in range(LAYERS):
        arrived(layer)
        lanes = slice(2 * layer * RANK, 2 * (layer + 1) * RANK)
        total = proj_ref[layer, :, : 2 * RANK].astype(F32)
        if layer > 1:
            before = (layer - 1) * RANK
            total = total + nn(hidden[:, :before], gram[:before, lanes])
        if layer > 0:
            near = slice((layer - 1) * RANK, layer * RANK)
            total = total + nn(hidden[:, near], gram[near, lanes])
        inverse = lax.rsqrt(square * (1.0 / WIDTH) + eps_norm)
        pre_act = total[:, :RANK] * inverse
        act = (pre_act * jax.nn.sigmoid(pre_act)).astype(BF)
        own = slice(layer * RANK, (layer + 1) * RANK)
        hidden[:, own] = act
        pre_saved[layer] = pre_act
        inv_saved[layer] = jnp.broadcast_to(inverse, (CHUNK, RANK))
        self_lanes = slice((2 * layer + 1) * RANK, 2 * (layer + 1) * RANK)
        leave_now = total[:, RANK:]
        leave_next = leave_now + nn(act, gram[own, self_lanes])
        leave_saved[layer] = leave_next
        square = jnp.maximum(
            square
            + jnp.sum(act.astype(F32) * (leave_now + leave_next), axis=1, keepdims=True),
            0.0,
        )
        rows_saved[layer] = wide.astype(BF)
        if layer == 0:
            for copy in copies:
                copy.wait()
        if layer < LAYERS - 1:
            wide = wide + nn(act, weights[layer % 2, layer // 2, RANK:, :])

    drain = jnp.zeros((CHUNK, 1), F32)
    incoming = grads_ref[...].astype(F32)
    for layer in range(LAYERS - 1, -1, -1):
        own = slice(layer * RANK, (layer + 1) * RANK)
        total = proj_ref[layer, :, 2 * RANK :].astype(F32)
        if layer < LAYERS - 2:
            lanes = slice(2 * (layer + 2) * RANK, 2 * LAYERS * RANK)
            total = total + nt(back[:, lanes], gram[own, lanes])
        if layer < LAYERS - 1:
            near = slice(2 * (layer + 1) * RANK, 2 * (layer + 2) * RANK)
            total = total + nt(back[:, near], gram[own, near])
        pre_act = pre_saved[layer]
        inverse = inv_saved[layer]
        hidden_grad = total - drain * leave_saved[layer]
        sig_act = jax.nn.sigmoid(pre_act)
        inner = hidden_grad * (sig_act * (1.0 + pre_act * (1.0 - sig_act)))
        inner = inner.astype(BF).astype(F32)
        unit = (inner * inverse).astype(BF)
        act = hidden[:, own]
        back[:, 2 * layer * RANK : (2 * layer + 1) * RANK] = unit
        back[:, (2 * layer + 1) * RANK : (2 * layer + 2) * RANK] = (
            -drain * act.astype(F32)
        ).astype(BF)
        share = (
            jnp.sum(inner * pre_act, axis=1, keepdims=True)
            * (inverse[:, :1] * inverse[:, :1])
            * (1.0 / WIDTH)
        )
        drain = drain + share
        layer_rows = rows_saved[layer]
        side = core if layer % 2 == 0 else 1 - core
        shares[side, layer // 2, :RANK, :] = tn(unit, layer_rows).astype(BF)
        shares[side, layer // 2, RANK:, :] = tn(act, incoming.astype(BF)).astype(BF)
        if layer > 0:
            incoming = (
                incoming
                + nn(unit, weights[layer % 2, layer // 2, :RANK, :])
                - share * layer_rows.astype(F32)
            )
        if layer % 2 == 0:
            for copy in leaving(layer // 2):
                copy.start()
    for half in range(HALF):
        for copy in leaving(half):
            copy.wait()


def chain(index, gram, proj, square, near, far, rows, grads):
    side = jax.ShapeDtypeStruct((HALF, 2 * RANK, SLICE), BF)
    return pl.pallas_call(
        chain_kernel,
        out_shape=(side, side),
        in_specs=[SMEM] + [ANY] * LAYERS + [VMEM, VMEM, ANY, ANY, VMEM, VMEM],
        out_specs=(ANY, ANY),
        scratch_shapes=[
            pltpu.VMEM((LAYERS * RANK, 2 * LAYERS * RANK), BF),
            pltpu.VMEM((2, HALF, 2 * RANK, SLICE), BF),
            pltpu.VMEM((2, HALF, 2 * RANK, SLICE), BF),
            pltpu.VMEM((CHUNK, LAYERS * RANK), BF),
            pltpu.VMEM((CHUNK, 2 * LAYERS * RANK), BF),
            pltpu.VMEM((LAYERS, CHUNK, RANK), F32),
            pltpu.VMEM((LAYERS, CHUNK, RANK), F32),
            pltpu.VMEM((LAYERS, CHUNK, SLICE), BF),
            pltpu.VMEM((LAYERS, CHUNK, RANK), F32),
            pltpu.SemaphoreType.DMA((LAYERS,)),
            pltpu.SemaphoreType.DMA((2,)),
            pltpu.SemaphoreType.DMA((2, HALF)),
        ],
        compiler_params=params(56),
        cost_estimate=cost(4 * 2**30, 20 * 2**20),
    )(index, *gram, proj, square, near, far, rows, grads)


def adam_update(weight, moment, second, grad):
    moment_new = beta_one * moment + (1.0 - beta_one) * grad
    second_new = beta_two * second + (1.0 - beta_two) * grad * grad
    corr_one = 1.0 - beta_one**step_count
    corr_two = 1.0 - beta_two**step_count
    weight_new = weight - rate * (moment_new / corr_one) / (
        jnp.sqrt(second_new / corr_two) + adam_eps
    )
    return (weight_new, moment_new, second_new)


def adam_kernel(parts_ref, gain_ref, *refs):
    ins, outs = refs[:6], refs[6:]
    total = jnp.sum(parts_ref[...].astype(F32), axis=0)
    grads = ((total[:RANK] * gain_ref[...]).T, total[RANK:])
    for first, grad in zip((0, 3), grads):
        updated = adam_update(*(ref[0] for ref in ins[first : first + 3]), grad)
        for ref, value in zip(outs[first : first + 3], updated):
            ref[0] = value


def adam(parts, gain, state):
    return pl.pallas_call(
        adam_kernel,
        out_shape=tuple(jax.ShapeDtypeStruct(value.shape, F32) for value in state),
        in_specs=[VMEM] * 8,
        out_specs=(VMEM,) * 6,
        compiler_params=params(32),
        cost_estimate=cost(2**22, 5 * 2**20),
    )(parts, gain, *state)


def per_device(
    micro_inputs,
    cotangent,
    norm_gain,
    enter_weight,
    enter_moment,
    enter_second,
    leave_weight,
    leave_moment,
    leave_second,
):
    section = lax.axis_index(SECTION)
    part = lax.axis_index(DP)
    core = lax.axis_index("c")
    index = jnp.stack([section, core, lax.axis_index("xh"), lax.axis_index("y")])
    gain = lax.dynamic_slice_in_dim(norm_gain, part * SLICE, SLICE, axis=1).astype(F32)
    swap = [(0, 1), (1, 0)]
    up = [(i, (i + 1) % 4) for i in range(4)]
    down = [(i, (i + 3) % 4) for i in range(4)]

    def exchange(value, axes):
        return lax.all_to_all(value, axes, split_axis=0, concat_axis=0, tiled=True)

    def spread(value):
        return exchange(jnp.broadcast_to(value[None], (PARTS,) + value.shape), DP)

    with jax.named_scope("weights"):
        near = exchange(own_weights(enter_weight, leave_weight, gain), ("xh", "y"))
        far = lax.ppermute(near, "c", swap)

    with jax.named_scope("gram"):
        both = jnp.concatenate(
            [
                lax.dynamic_slice_in_dim(
                    value.reshape(CHUNK, WIDTH), section * OWN_ROWS, OWN_ROWS, 0
                )
                for value in (micro_inputs, cotangent)
            ]
        )
        packed = exchange(gram_and_rows(index, near, far, both), DP)
        blocks = spread(jnp.sum(packed[:, :PIECE, :].astype(F32), axis=0).astype(BF))
        blocks = blocks.reshape(HALF, RANK, LANES)
        other = lax.ppermute(blocks, "xh", swap)

    with jax.named_scope("project"):
        proj, rows, grads, square = project(index, packed, near, far)

        def ring(value):
            below = lax.ppermute(value, "y", up)
            above = lax.ppermute(value, "y", down)
            return [value, above, lax.ppermute(above, "y", down), below]

        plane = ring(blocks)
        other, _ = lax.optimization_barrier((other, proj))
        gram = plane + ring(other)
        gram = gram + [lax.ppermute(value, "c", swap) for value in gram]
        proj, _, _ = lax.optimization_barrier((exchange(proj, DP), other, plane[2]))
        proj = spread(jnp.sum(proj.astype(F32), axis=0).astype(BF))

    with jax.named_scope("chain"):
        keep, other = chain(index, gram, proj, square, near, far, rows, grads)

    with jax.named_scope("sum"):
        received = lax.ppermute(other, "c", swap)
        parts = exchange((keep.astype(F32) + received.astype(F32)).astype(BF), ("xh", "y"))

    with jax.named_scope("adam"):
        return adam(
            parts,
            gain,
            (enter_weight, enter_moment, enter_second, leave_weight, leave_moment, leave_second),
        )


def solution(mesh):
    split = Mesh(mesh.devices.reshape(2, 4, 2, 2, 8), SECTION + DP)
    rows = P(None, None, DP, None)
    enter = P(SECTION, DP, None)
    leave = P(SECTION, None, DP)
    return jax.shard_map(
        per_device,
        mesh=split,
        in_specs=(rows, rows, P(SECTION, None)) + (enter,) * 3 + (leave,) * 3,
        out_specs=(enter,) * 3 + (leave,) * 3,
        check_vma=False,
    )
```
